32 devices in a mesh: blk: 8 (over y, x, core), shard: 4 (over z).
Axes of the slice: x: 2, y: 2, z: 4, core: 2. Of those that a mesh axis runs over, the one named last changes fastest.
Arguments:
- queries: bfloat16 [2048, 2560], P('blk', 'shard'), may hold values from -256 to 256
- key_rows: bfloat16 [2048, 2560], P('blk', 'shard'), may hold values from -6 to 6
- values: bfloat16 [2048, 2560], P('blk', 'shard'), may hold values from -6 to 6
- segment_ids: int32 [8, 256], P('blk'), may hold values from 0 to 3, never falling along the last dimension, each value on 1 to 128 neighbouring positions
- residual: bfloat16 [2048, 2560], P('blk', 'shard'), may hold values from -6 to 6
- out_weight: bfloat16 [2560, 2560], P('shard', 'blk'), may hold values from -0.125 to 0.125
- cotangent: bfloat16 [2048, 2560], P('blk', 'shard'), may hold values from -6 to 6
Outputs:
- layer_out: bfloat16 [2048, 2560], P('blk', 'shard')
- weight_grad: float32 [2560, 2560], P('blk', 'shard')
- query_grad: bfloat16 [2048, 2560], P('blk', 'shard')
- key_grad: bfloat16 [2048, 2560], P('blk', 'shard')
- value_grad: bfloat16 [2048, 2560], P('blk', 'shard')
The draws below stay inside these ranges and needn't reach their ends.
Inputs may be any that keep to these rules, and one draw needn't show every extreme that they name: `segment_ids`: in each worker's row the document numbers never fall, and each document has 1 to 128 tokens.
All inputs are finite; a program needn't handle non-finite values.
Results may differ from the reference program's by a relative error of at most 0.0059.
Values may be sent and summed in bfloat16 or wider, within the bound.
No kernel may reach another device: no remote copies, remote signals or barrier semaphores. Data moves between devices by JAX's collectives and lax.ppermute only.
A program may use at most 128 MiB of HBM per device.

```python
import math
import jax
import jax.numpy as jnp
import numpy as np
from jax import lax

DW = 2560
HEADS = 20
HEAD = 128
TOK_DEV = 256
HD = 2560
WORKERS = 8
TOKENS = 2048


def shared_rows(key):
    base = jax.random.normal(key, (TOKENS, HEADS * HEAD), jnp.float32)
    return jnp.clip(base, -6.0, 6.0)


def draw_key_rows(key, part):
    keys_base = shared_rows(key)
    return keys_base.astype(jnp.bfloat16)


def draw_queries(key, part):
    key = jax.random.fold_in(key, 5)
    own = jnp.clip(jax.random.normal(key, (TOKENS, HEADS * HEAD), jnp.float32), -6.0, 6.0)
    return own.astype(jnp.bfloat16)


def strengthened(entries, key, source, target, blocks, factor):
    def block_of(position):
        return (jnp.arange(entries.shape[position]) // (entries.shape[position] // blocks)).reshape((-1,) + (1,) * (entries.ndim - 1 - position))

    first = jax.random.permutation(key, blocks)[block_of(target)]
    far = (block_of(target) + blocks // 2) % blocks
    return jnp.where((block_of(source) == first) | (block_of(source) == far), factor * entries, entries)


def level_of(rng, extent, cuts, low, largest):
    def one(dim, blocks):
        draws = jax.random.uniform(jax.random.fold_in(jax.random.fold_in(rng, 6), dim), (blocks,), jnp.float32, low / len(cuts), largest / len(cuts))
        return jnp.repeat(jnp.exp(draws), extent[dim] // blocks).reshape((-1,) + (1,) * (len(extent) - dim - 1))

    gain = one(*cuts[0])
    for cut in cuts[1:]:
        gain = gain * one(*cut)
    return gain


def length_profile(amount, total, bound, slope):
    weights = [(1 << 20) // math.isqrt(standing ** slope) + 1 for standing in range(2, amount + 1)]
    rest, holding = total - bound - (amount - 1), [1] * (amount - 1)
    while rest > 0:
        candidates = [i for i in range(amount - 1) if holding[i] < bound]
        mass, remaining = sum([weights[i] for i in candidates]), rest
        for i in candidates:
            addition = min(bound - holding[i], max(1, remaining * weights[i] // mass), rest)
            holding[i] = holding[i] + addition
            rest = rest - addition
    return np.array([bound] + holding)


def ragged(rng, number_of, total, reach, slope):
    if number_of == 2:
        one = jax.random.randint(rng, (), max(1, total - reach), min(reach, total - 1) + 1)
        return jnp.stack([one, total - one])
    lengths = jnp.asarray(length_profile(number_of, total, reach, slope), jnp.int32)
    twos = (number_of - 1) // 2
    donor, sink = lengths[1:1 + 2 * twos:2], lengths[2:2 + 2 * twos:2]
    margin = jnp.minimum(donor - 1, reach - sink)
    passed = jax.random.randint(jax.random.fold_in(rng, 1), (twos,), 0, 1 << 20) % (margin + 1)
    lengths = lengths.at[1:1 + 2 * twos:2].set(donor - passed).at[2:2 + 2 * twos:2].set(sink + passed)
    return lengths[jax.random.permutation(jax.random.fold_in(rng, 2), number_of)]


def bell_draw(own_key, dims, scale, reach, shards=(), held_as=jnp.bfloat16):
    gain = level_of(own_key, dims, shards, -0.22, 0.18) if shards else 1.0
    entries = jax.random.normal(own_key, dims, jnp.float32) * scale * gain
    return jnp.minimum(jnp.maximum(entries, -reach), reach).astype(held_as)


def bell_draw_with(stream_key, shape, scale, bound, cuts, heavy, kind=jnp.bfloat16):
    array = scale * jax.random.normal(stream_key, shape, jnp.float32)
    if cuts:
        array = array * level_of(stream_key, shape, cuts, -0.22, 0.18)
    return jnp.clip(strengthened(array, jax.random.fold_in(stream_key, 3), *heavy), -bound, bound).astype(kind)


def setup_inputs(seed: int = 0) -> dict:
    seeds = jax.random.split(jax.random.key(seed), 8)
    queries = draw_queries(jax.random.fold_in(seeds[7], 71), 0)
    key_rows = draw_key_rows(jax.random.fold_in(seeds[7], 71), 0)
    values = bell_draw(seeds[2], (TOKENS, HD), 1.0, 6.0, ((0, 8), (1, 4)))
    segment_ids = jax.vmap(lambda own: jnp.searchsorted(jnp.cumsum(ragged(own, 4, TOK_DEV, TOK_DEV // 2, 0)), jnp.arange(TOK_DEV), side="right"))(jax.random.split(seeds[3], WORKERS)).reshape((WORKERS, TOK_DEV)).astype(jnp.int32)
    residual = bell_draw(seeds[4], (TOKENS, DW), 1.0, 6.0, ((0, 8), (1, 4)))
    out_weight = bell_draw(seeds[5], (HD, DW), HD ** -0.5, 0.125, ((0, 4), (1, 8)))
    cotangent = bell_draw_with(seeds[6], (TOKENS, DW), 1.0, 6.0, ((0, 8), (1, 4)), (0, 1, 8, 2.0))
    return dict(queries=queries, key_rows=key_rows, values=values, segment_ids=segment_ids, residual=residual, out_weight=out_weight, cotangent=cotangent)


masked_fill = -1e+30

def attention_probs(q_three, k_three, seg_row):
    count = q_three.shape[0]
    scores = jnp.einsum('qhd,khd->hqk', q_three.astype(jnp.float32), k_three.astype(jnp.float32))
    scores = scores * (1.0 / math.sqrt(HEAD))
    places = jnp.arange(count, dtype=jnp.int32)
    allowed = (places[None, :] <= places[:, None]) & (seg_row[None, :] == seg_row[:, None])
    scores = jnp.where(allowed[None], scores, masked_fill)
    highest = lax.optimization_barrier(jnp.max(scores, axis=-1, keepdims=True))
    weights = jnp.exp(scores - highest)
    return weights / lax.optimization_barrier(jnp.sum(weights, axis=-1, keepdims=True))

def reference(queries, key_rows, values, segment_ids, residual, out_weight, cotangent):
    split_shape = (WORKERS, TOK_DEV, HEADS, HEAD)
    q_all = queries.reshape(split_shape)
    k_all = key_rows.reshape(split_shape)
    v_all = values.reshape(split_shape)

    def forward_one(items):
        q_three, k_three, v_three, seg_row = items
        probs = attention_probs(q_three, k_three, seg_row)
        p_low = probs.astype(jnp.bfloat16)
        mixed = jnp.einsum('hqk,khd->qhd', p_low.astype(jnp.float32), v_three.astype(jnp.float32))
        return mixed.reshape(TOK_DEV, HD).astype(jnp.bfloat16)
    context = lax.map(forward_one, (q_all, k_all, v_all, segment_ids)).reshape(TOKENS, HD)
    projected = jnp.dot(context, out_weight, preferred_element_type=jnp.float32)
    layer_out = (residual.astype(jnp.float32) + projected).astype(jnp.bfloat16)
    d_context = jnp.dot(cotangent, out_weight.T, preferred_element_type=jnp.float32).astype(jnp.bfloat16)
    weight_grad = jnp.dot(cotangent.T, context, preferred_element_type=jnp.float32) * (1.0 / math.sqrt(TOKENS))
    dctx_all = d_context.reshape(split_shape)

    def backward_one(items):
        q_three, k_three, v_three, seg_row, dctx_three = items
        probs = attention_probs(q_three, k_three, seg_row)
        p_low = probs.astype(jnp.bfloat16)
        dctx_f = dctx_three.astype(jnp.float32)
        d_probs = jnp.einsum('qhd,khd->hqk', dctx_f, v_three.astype(jnp.float32))
        v_grad = jnp.einsum('hqk,qhd->khd', p_low.astype(jnp.float32), dctx_f)
        inner = lax.optimization_barrier(jnp.sum(probs * d_probs, axis=-1, keepdims=True))
        d_scores = (probs * (d_probs - inner)).astype(jnp.bfloat16).astype(jnp.float32)
        scale = 1.0 / math.sqrt(HEAD)
        q_grad = jnp.einsum('hqk,khd->qhd', d_scores, k_three.astype(jnp.float32)) * scale
        k_grad = jnp.einsum('hqk,qhd->khd', d_scores, q_three.astype(jnp.float32)) * scale
        return (q_grad.reshape(TOK_DEV, HD).astype(jnp.bfloat16), k_grad.reshape(TOK_DEV, HD).astype(jnp.bfloat16), v_grad.reshape(TOK_DEV, HD).astype(jnp.bfloat16))
    q_grad, k_grad, v_grad = lax.map(backward_one, (q_all, k_all, v_all, segment_ids, dctx_all))
    return (layer_out, weight_grad, q_grad.reshape(TOKENS, HD), k_grad.reshape(TOKENS, HD), v_grad.reshape(TOKENS, HD))
```

```python
import math

import jax
import jax.numpy as jnp
from jax import lax
from jax.experimental import pallas as pl
from jax.experimental.pallas import tpu as pltpu
from jax.sharding import PartitionSpec as P

HEAD = 128
MASKED = -1e30
F32 = jnp.float32
BF16 = jnp.bfloat16
NT = (((1,), (1,)), ((), ()))
NN = (((1,), (0,)), ((), ()))
TN = (((0,), (0,)), ((), ()))


def dot(a, b, dims):
    return lax.dot_general(a, b, dims, preferred_element_type=F32)


def call(kernel, outs, *args, flops=0):
    size = sum(math.prod(o.shape) * o.dtype.itemsize for o in (*outs, *args))
    return pl.pallas_call(
        kernel,
        out_shape=tuple(outs),
        in_specs=[pl.BlockSpec(memory_space=pltpu.VMEM)] * len(args),
        out_specs=tuple([pl.BlockSpec(memory_space=pltpu.VMEM)] * len(outs)),
        compiler_params=pltpu.CompilerParams(vmem_limit_bytes=40 * 1024 * 1024),
        cost_estimate=pl.CostEstimate(flops=flops, bytes_accessed=size, transcendentals=0),
    )(*args)


def shape(*dims, dtype=BF16):
    return jax.ShapeDtypeStruct(dims, dtype)


def visible_mask(seg_ref):
    count = seg_ref.shape[1]
    seg = jnp.broadcast_to(seg_ref[...].astype(F32), (count, count))
    rows = lax.broadcasted_iota(jnp.int32, (count, count), 0)
    cols = lax.broadcasted_iota(jnp.int32, (count, count), 1)
    return (cols <= rows) & (seg == seg.T)


def head_probs(q, k, allowed):
    scores = dot(q, k, NT) * (1.0 / math.sqrt(HEAD))
    scores = jnp.where(allowed, scores, MASKED)
    weights = jnp.exp(scores - jnp.max(scores, axis=-1, keepdims=True))
    return weights / jnp.sum(weights, axis=-1, keepdims=True)


def forward_kernel(q_ref, k_ref, v_ref, seg_ref, ctx_ref):
    allowed = visible_mask(seg_ref)
    for h in range(q_ref.shape[1] // HEAD):
        at = pl.ds(h * HEAD, HEAD)
        probs = head_probs(q_ref[:, at], k_ref[:, at], allowed).astype(BF16)
        ctx_ref[:, at] = dot(probs, v_ref[:, at], NN).astype(BF16)


def backward_kernel(q_ref, k_ref, v_ref, seg_ref, mine_ref, other_ref, dq_ref, dk_ref, dv_ref):
    allowed = visible_mask(seg_ref)
    scale = 1.0 / math.sqrt(HEAD)
    for h in range(q_ref.shape[1] // HEAD):
        at = pl.ds(h * HEAD, HEAD)
        q, k, v = q_ref[:, at], k_ref[:, at], v_ref[:, at]
        probs = head_probs(q, k, allowed)
        d_ctx = (mine_ref[:, at] + other_ref[:, at].astype(F32)).astype(BF16)
        d_probs = dot(d_ctx, v, NT)
        dv_ref[:, at] = dot(probs.astype(BF16), d_ctx, TN).astype(BF16)
        inner = jnp.sum(probs * d_probs, axis=-1, keepdims=True)
        d_scores = (probs * (d_probs - inner)).astype(BF16)
        dq_ref[:, at] = (dot(d_scores, k, NN) * scale).astype(BF16)
        dk_ref[:, at] = (dot(d_scores, q, TN) * scale).astype(BF16)


def plane_slot(plane, group):
    return plane ^ (lax.axis_index("blk") // group)


def unit_kernel(own_ref, other_ref, unit_ref):
    half, count = unit_ref.shape[0], own_ref.shape[0]
    core = lax.rem(lax.axis_index("blk"), 2)
    own, other = own_ref[...].T, other_ref[...].T
    for side in range(2):

        @pl.when(core == side)
        def _():
            rows = slice(side * half, (side + 1) * half)
            unit_ref[:, :count] = own[rows]
            unit_ref[:, count:] = other[rows]


def make_unit(own, other, strips):
    count, width = own.shape
    half = width // 2
    if strips == 1:
        return call(unit_kernel, (shape(half, 2 * count),), own, other)[0]
    core = lax.rem(lax.axis_index("blk"), 2)
    both = jnp.concatenate([own, other], axis=0).T.reshape(strips, 2, half // strips, 2 * count)
    return lax.dynamic_index_in_dim(both, core, 1, keepdims=False).reshape(half, 2 * count)


def project_kernel(sign, away, group, has_past, *refs):
    w_ref, own_ref, other_ref = refs[:3]
    past_ref, out_ref = (refs[3], refs[4]) if has_past else (None, refs[3])
    planes, count = w_ref.shape[0], own_ref.shape[0]
    z = lax.axis_index("shard")
    plane = z + sign * away

    @pl.when((plane >= 0) & (plane < planes))
    def _():
        w = w_ref[plane_slot(plane, group)]
        for i, ctx_ref in enumerate((own_ref, other_ref)):
            at = pl.ds(i * count, count)
            part = dot(w, ctx_ref[...], NT)
            if has_past:
                before = z - sign
                live = (before >= 0) & (before < planes)
                part = part + jnp.where(live, past_ref[:, at].astype(F32), 0.0)
            out_ref[:, at] = part.astype(BF16)


def project(sign, away, group, w, own, other, past):
    args = (w, own, other) + (() if past is None else (past,))
    out = shape(w.shape[1], 2 * own.shape[0])

    def kernel(*refs):
        project_kernel(sign, away, group, past is not None, *refs)

    return call(kernel, (out,), *args, flops=2 * math.prod(out.shape) * w.shape[2])[0]


def last_project_kernel(group, w_ref, own_ref, other_ref, up_ref, down_ref, keep_ref, send_ref):
    planes, count = w_ref.shape[0], own_ref.shape[0]
    z = lax.axis_index("shard")
    w = w_ref[plane_slot(z, group)]
    for i, (ctx_ref, out_ref) in enumerate(((own_ref, keep_ref), (other_ref, send_ref))):
        at = pl.ds(i * count, count)
        part = dot(w, ctx_ref[...], NT)
        part = part + jnp.where(z > 0, up_ref[:, at].astype(F32), 0.0)
        out_ref[...] = part + jnp.where(z < planes - 1, down_ref[:, at].astype(F32), 0.0)


def layer_out_kernel(residual_ref, keep_ref, other_ref, out_ref):
    half = keep_ref.shape[0]
    core = lax.rem(lax.axis_index("blk"), 2)
    keep, other = keep_ref[...], other_ref[...]
    for side, order in enumerate(((keep, other), (other, keep))):

        @pl.when(core == side)
        def _():
            total = jnp.concatenate(order, axis=0).T
            out_ref[...] = (residual_ref[...].astype(F32) + total).astype(BF16)


def make_layer_out(residual, keep, other, strips):
    count, width = residual.shape
    if strips == 1:
        return call(layer_out_kernel, (shape(count, width),), residual, keep, other)[0]
    core = lax.rem(lax.axis_index("blk"), 2)
    pair = jnp.stack([keep, other]).reshape(2, strips, -1, count)
    pair = jnp.where(core == 0, pair, pair[::-1])
    total = pair.transpose(1, 0, 2, 3).reshape(width, count)
    return (residual.astype(F32) + total.T).astype(BF16)


def for_each_plane(unit_refs, planes, body):
    z = lax.axis_index("shard")
    steps = [0] + [-k for k in range(1, planes)] + list(range(1, planes))
    for step, unit_ref in zip(steps, unit_refs):
        if step == 0:
            body(z, unit_ref)
        else:
            plane = z + step
            pl.when((plane >= 0) & (plane < planes))(lambda p=plane, u=unit_ref: body(p, u))


def d_context_kernel(group, *refs):
    *unit_refs, w_ref, mine_ref, send_ref, total = refs
    count = mine_ref.shape[0]
    total[...] = jnp.zeros_like(total)

    def body(plane, unit_ref):
        total[...] += dot(unit_ref[...], w_ref[plane_slot(plane, group)], TN)

    for_each_plane(unit_refs, w_ref.shape[0], body)
    mine_ref[...] = total[:count]
    send_ref[...] = total[count:].astype(BF16)


def weight_grad_kernel(group, planes, *refs):
    *unit_refs, own_ref, other_ref, send_a, send_b, keep_a, keep_b = refs
    count, rows = own_ref.shape[0], send_a.shape[1]

    def body(plane, unit_ref):
        slot = plane_slot(plane, group)
        part = dot(unit_ref[:, :count], own_ref[...], NN)
        part = part + dot(unit_ref[:, count:], other_ref[...], NN)
        low, high = slot & 1, slot >> 1
        first, second = part[:rows], part[rows:]

        @pl.when(low == 1)
        def _():
            send_a[high] = first.astype(BF16)

        @pl.when(low == 0)
        def _():
            keep_a[high] = first

        @pl.when(high == 1)
        def _():
            send_b[low] = second.astype(BF16)

        @pl.when(high == 0)
        def _():
            keep_b[low] = second

    for_each_plane(unit_refs, planes, body)


def half_sum_kernel(keep_a, keep_b, from_a, from_b, send_a, send_b, left_a, left_b):
    send_a[...] = (keep_a[1] + from_a[1].astype(F32)).astype(BF16)
    send_b[...] = (keep_b[1] + from_b[1].astype(F32)).astype(BF16)
    left_a[...] = keep_a[0] + from_a[0].astype(F32)
    left_b[...] = keep_b[0] + from_b[0].astype(F32)


def grad_sum_kernel(scale, left_a, left_b, from_a, from_b, out_ref):
    rows = left_a.shape[0]
    out_ref[:rows] = (left_a[...] + from_a[...].astype(F32)) * scale
    out_ref[rows:] = (left_b[...] + from_b[...].astype(F32)) * scale


def solution(mesh):
    blk, planes = mesh.shape["blk"], mesh.shape["shard"]
    chips = blk // 2
    strips = chips // planes

    def swap(value, bit):
        return lax.ppermute(value, "blk", [(i, i ^ bit) for i in range(blk)])

    def pass_up(value, first, last):
        return lax.ppermute(value, "shard", [(i, i + 1) for i in range(first, last)])

    def pass_down(value, first, last):
        return lax.ppermute(value, "shard", [(i, i - 1) for i in range(first, last, -1)])

    def per_device(queries, key_rows, values, segment_ids, residual, out_weight, cotangent):
        count = queries.shape[0]
        width = queries.shape[1]
        half = width // 2
        position = lax.axis_index("blk") // 2
        group = 2 * strips

        w_own = out_weight.T
        bit = 1
        while bit < strips:
            there = swap(w_own, 2 * bit)
            upper = (position // bit) % 2
            w_own = jnp.concatenate(
                [jnp.where(upper, there, w_own), jnp.where(upper, w_own, there)], axis=0
            )
            bit *= 2
        cut = half // 2
        a_own, b_own = w_own[:cut], w_own[cut:]
        a_one = swap(a_own, group)
        b_two = swap(b_own, 2 * group)
        cot_other = swap(cotangent, 1)
        a_pair = jnp.stack([a_own, a_one])
        b_pair = jnp.stack([b_own, b_two])
        a_high = swap(a_pair, 2 * group)
        b_low = swap(b_pair, group)
        w_all = jnp.concatenate(
            [
                jnp.concatenate([a_pair, a_high], axis=0),
                jnp.stack([b_own, b_low[0], b_two, b_low[1]]),
            ],
            axis=1,
        )

        unit = make_unit(cotangent, cot_other, strips)
        ups, downs, last = [unit], [unit], planes - 1
        for k in range(1, planes):
            ups.append(pass_up(ups[-1], k - 1, last))
            downs.append(pass_down(downs[-1], last - k + 1, 0))
        units = [unit, *ups[1:], *downs[1:]]

        ctx = call(
            forward_kernel,
            (shape(count, width),),
            queries,
            key_rows,
            values,
            segment_ids,
            flops=4 * count * count * width,
        )[0]
        ctx_other = swap(ctx, 1)

        up = down = None
        for away in range(planes - 1, 0, -1):
            up = project(1, away, group, w_all, ctx, ctx_other, up)
            down = project(-1, away, group, w_all, ctx, ctx_other, down)
            up = pass_up(up, 0, planes - away)
            down = pass_down(down, last, away - 1)

        def last_project(*refs):
            last_project_kernel(group, *refs)

        keep, send = call(
            last_project,
            (shape(half, count, dtype=F32),) * 2,
            w_all,
            ctx,
            ctx_other,
            up,
            down,
            flops=4 * half * count * width,
        )
        layer_out = make_layer_out(residual, keep, swap(send, 1), strips)

        def d_context(*refs):
            d_context_kernel(group, *refs)

        mine, send = pl.pallas_call(
            d_context,
            out_shape=(shape(count, width, dtype=F32), shape(count, width)),
            in_specs=[pl.BlockSpec(memory_space=pltpu.VMEM)] * (len(units) + 1),
            out_specs=(pl.BlockSpec(memory_space=pltpu.VMEM),) * 2,
            scratch_shapes=[pltpu.VMEM((2 * count, width), F32)],
            compiler_params=pltpu.CompilerParams(vmem_limit_bytes=40 * 1024 * 1024),
            cost_estimate=pl.CostEstimate(
                flops=4 * count * width * half * planes, bytes_accessed=1 << 23, transcendentals=0
            ),
        )(*units, w_all)
        d_ctx_other = swap(send, 1)

        def weight_parts(*refs):
            weight_grad_kernel(group, planes, *refs)

        send_a, send_b, keep_a, keep_b = call(
            weight_parts,
            (shape(2, cut, width),) * 2 + (shape(2, cut, width, dtype=F32),) * 2,
            *units,
            ctx,
            ctx_other,
            flops=4 * count * width * half * planes,
        )
        from_a, from_b = swap(send_a, group), swap(send_b, 2 * group)
        send_a, send_b, left_a, left_b = call(
            half_sum_kernel,
            (shape(cut, width),) * 2 + (shape(cut, width, dtype=F32),) * 2,
            keep_a,
            keep_b,
            from_a,
            from_b,
        )
        from_a, from_b = swap(send_a, 2 * group), swap(send_b, group)
        grad_scale = 1.0 / math.sqrt(count * blk)

        def grad_sum(*refs):
            grad_sum_kernel(grad_scale, *refs)

        total = call(
            grad_sum, (shape(half, width, dtype=F32),), left_a, left_b, from_a, from_b
        )[0]
        bit = strips // 2
        while bit >= 1:
            lower, upper = jnp.split(total, 2, axis=0)
            right = (position // bit) % 2
            sent = jnp.where(right, lower, upper)
            total = jnp.where(right, upper, lower) + swap(sent, 2 * bit)
            bit //= 2

        d_queries, d_keys, d_values = call(
            backward_kernel,
            (shape(count, width),) * 3,
            queries,
            key_rows,
            values,
            segment_ids,
            mine,
            d_ctx_other,
            flops=10 * count * count * width,
        )
        return layer_out, total, d_queries, d_keys, d_values

    spread = P("blk", "shard")
    return jax.shard_map(
        per_device,
        mesh=mesh,
        in_specs=(spread, spread, spread, P("blk", None), spread, P("shard", "blk"), spread),
        out_specs=(spread,) * 5,
        check_vma=False,
    )
```

```python
import math

import jax
import jax.numpy as jnp
from jax import lax
from jax.experimental import pallas as pl
from jax.experimental.pallas import tpu as pltpu
from jax.sharding import PartitionSpec as P

HEAD = 128
MASKED = -1e30
F32 = jnp.float32
BF16 = jnp.bfloat16
NT = (((1,), (1,)), ((), ()))
NN = (((1,), (0,)), ((), ()))
TN = (((0,), (0,)), ((), ()))


def dot(a, b, dims):
    return lax.dot_general(a, b, dims, preferred_element_type=F32)


def call(kernel, outs, *args, flops=0):
    size = sum(math.prod(o.shape) * o.dtype.itemsize for o in (*outs, *args))
    return pl.pallas_call(
        kernel,
        out_shape=tuple(outs),
        in_specs=[pl.BlockSpec(memory_space=pltpu.VMEM)] * len(args),
        out_specs=tuple([pl.BlockSpec(memory_space=pltpu.VMEM)] * len(outs)),
        compiler_params=pltpu.CompilerParams(vmem_limit_bytes=40 * 1024 * 1024),
        cost_estimate=pl.CostEstimate(flops=flops, bytes_accessed=size, transcendentals=0),
    )(*args)


def shape(*dims, dtype=BF16):
    return jax.ShapeDtypeStruct(dims, dtype)


def visible_mask(seg_ref):
    count = seg_ref.shape[1]
    seg = jnp.broadcast_to(seg_ref[...].astype(F32), (count, count))
    rows = lax.broadcasted_iota(jnp.int32, (count, count), 0)
    cols = lax.broadcasted_iota(jnp.int32, (count, count), 1)
    return (cols <= rows) & (seg == seg.T)


def head_probs(q, k, allowed):
    scores = dot(q, k, NT) * (1.0 / math.sqrt(HEAD))
    scores = jnp.where(allowed, scores, MASKED)
    weights = jnp.exp(scores - jnp.max(scores, axis=-1, keepdims=True))
    return weights / jnp.sum(weights, axis=-1, keepdims=True)


def forward_kernel(q_ref, k_ref, v_ref, seg_ref, ctx_ref, probs_ref):
    allowed = visible_mask(seg_ref)
    for h in range(q_ref.shape[1] // HEAD):
        at = pl.ds(h * HEAD, HEAD)
        probs = head_probs(q_ref[:, at], k_ref[:, at], allowed)
        probs_ref[h] = probs
        ctx_ref[:, at] = dot(probs.astype(BF16), v_ref[:, at], NN).astype(BF16)


def backward_kernel(q_ref, k_ref, v_ref, probs_ref, mine_ref, other_ref, dq_ref, dk_ref, dv_ref):
    scale = 1.0 / math.sqrt(HEAD)
    for h in range(q_ref.shape[1] // HEAD):
        at = pl.ds(h * HEAD, HEAD)
        q, k, v = q_ref[:, at], k_ref[:, at], v_ref[:, at]
        probs = probs_ref[h]
        d_ctx = (mine_ref[:, at] + other_ref[:, at].astype(F32)).astype(BF16)
        d_probs = dot(d_ctx, v, NT)
        dv_ref[:, at] = dot(probs.astype(BF16), d_ctx, TN).astype(BF16)
        inner = jnp.sum(probs * d_probs, axis=-1, keepdims=True)
        d_scores = (probs * (d_probs - inner)).astype(BF16)
        dq_ref[:, at] = (dot(d_scores, k, NN) * scale).astype(BF16)
        dk_ref[:, at] = (dot(d_scores, q, TN) * scale).astype(BF16)


def plane_slot(plane, group):
    return plane ^ (lax.axis_index("blk") // group)


def unit_kernel(own_ref, other_ref, unit_ref):
    half, count = unit_ref.shape[0], own_ref.shape[0]
    core = lax.rem(lax.axis_index("blk"), 2)
    own, other = own_ref[...].T, other_ref[...].T
    for side in range(2):

        @pl.when(core == side)
        def _():
            rows = slice(side * half, (side + 1) * half)
            unit_ref[:, :count] = own[rows]
            unit_ref[:, count:] = other[rows]


def make_unit(own, other, strips):
    count, width = own.shape
    half = width // 2
    if strips == 1:
        return call(unit_kernel, (shape(half, 2 * count),), own, other)[0]
    core = lax.rem(lax.axis_index("blk"), 2)
    both = jnp.concatenate([own, other], axis=0).T.reshape(strips, 2, half // strips, 2 * count)
    return lax.dynamic_index_in_dim(both, core, 1, keepdims=False).reshape(half, 2 * count)


def is_inner(z):
    return (z == 1) | (z == 2)


def project_part(w_ref, ctx_ref, plane, group):
    return dot(w_ref[plane_slot(plane, group)], ctx_ref[...], NT)


def first_message_kernel(group, w_ref, own_ref, other_ref, passing_ref, out_ref):
    count = own_ref.shape[0]
    z = lax.axis_index("shard")

    @pl.when(is_inner(z))
    def _():
        out_ref[...] = passing_ref[...]

    @pl.when(~is_inner(z))
    def _():
        for i, ctx_ref in enumerate((own_ref, other_ref)):
            part = project_part(w_ref, ctx_ref, z ^ 3, group)
            out_ref[:, pl.ds(i * count, count)] = part.astype(BF16)


def message_kernel(flip, group, w_ref, own_ref, other_ref, past_ref, out_ref):
    count = own_ref.shape[0]
    z = lax.axis_index("shard")
    for i, ctx_ref in enumerate((own_ref, other_ref)):
        at = pl.ds(i * count, count)
        part = project_part(w_ref, ctx_ref, z ^ flip, group)
        past = jnp.where(is_inner(z), past_ref[:, at].astype(F32), 0.0)
        out_ref[:, at] = (part + past).astype(BF16)


def last_project_kernel(group, w_ref, own_ref, other_ref, pair_ref, mid_ref, keep_ref, send_ref):
    count = own_ref.shape[0]
    z = lax.axis_index("shard")
    for i, (ctx_ref, out_ref) in enumerate(((own_ref, keep_ref), (other_ref, send_ref))):
        at = pl.ds(i * count, count)
        part = project_part(w_ref, ctx_ref, z, group) + pair_ref[:, at].astype(F32)
        out_ref[...] = part + jnp.where(is_inner(z), mid_ref[:, at].astype(F32), 0.0)


def layer_out_kernel(residual_ref, keep_ref, other_ref, out_ref):
    half = keep_ref.shape[0]
    core = lax.rem(lax.axis_index("blk"), 2)
    keep, other = keep_ref[...], other_ref[...]
    for side, order in enumerate(((keep, other), (other, keep))):

        @pl.when(core == side)
        def _():
            total = jnp.concatenate(order, axis=0).T
            out_ref[...] = (residual_ref[...].astype(F32) + total).astype(BF16)


def make_layer_out(residual, keep, other, strips):
    count, width = residual.shape
    if strips == 1:
        return call(layer_out_kernel, (shape(count, width),), residual, keep, other)[0]
    core = lax.rem(lax.axis_index("blk"), 2)
    pair = jnp.stack([keep, other]).reshape(2, strips, -1, count)
    pair = jnp.where(core == 0, pair, pair[::-1])
    total = pair.transpose(1, 0, 2, 3).reshape(width, count)
    return (residual.astype(F32) + total.T).astype(BF16)


def early_planes(unit_ref, near_ref, outer_ref, inner_ref, body):
    z = lax.axis_index("shard")
    body(z, unit_ref)
    body(z ^ 1, near_ref)
    pl.when(is_inner(z))(lambda: body(z ^ 2, inner_ref))
    pl.when(~is_inner(z))(lambda: body(z ^ 2, outer_ref))


def late_plane(inner_ref, outer_ref, body):
    z = lax.axis_index("shard")
    pl.when(is_inner(z))(lambda: body(z ^ 3, inner_ref))
    pl.when(~is_inner(z))(lambda: body(z ^ 3, outer_ref))


def d_context_early_kernel(group, *refs):
    *unit_refs, w_ref, total_ref = refs
    total_ref[...] = jnp.zeros_like(total_ref)

    def body(plane, unit_ref):
        total_ref[...] += dot(unit_ref[...], w_ref[plane_slot(plane, group)], TN)

    early_planes(*unit_refs, body)


def d_context_late_kernel(group, *refs):
    inner_ref, outer_ref, w_ref, total_ref, mine_ref, send_ref = refs
    count = mine_ref.shape[0]

    def body(plane, unit_ref):
        part = dot(unit_ref[...], w_ref[plane_slot(plane, group)], TN)
        mine_ref[...] = total_ref[:count] + part[:count]
        send_ref[...] = (total_ref[count:] + part[count:]).astype(BF16)

    late_plane(inner_ref, outer_ref, body)


def weight_part(unit_ref, own_ref, other_ref):
    count = own_ref.shape[0]
    part = dot(unit_ref[:, :count], own_ref[...], NN)
    return part + dot(unit_ref[:, count:], other_ref[...], NN)


def late_slot(group):
    return plane_slot(lax.axis_index("shard") ^ 3, group)


def choose(condition, then, other):
    pl.when(condition)(then)
    pl.when(~condition)(other)


def weight_early_kernel(group, *refs):
    *unit_refs, own_ref, other_ref, send_a, send_b, keep_a, keep_b, rest_a, rest_b = refs
    rows = rest_a.shape[0]
    late = late_slot(group)

    def body(plane, unit_ref):
        slot = plane_slot(plane, group)
        part = weight_part(unit_ref, own_ref, other_ref)

        def place(block, bit, send, keep, rest):
            def into_rest():
                rest[...] = block

            def into_send():
                send[...] = block.astype(BF16)

            def into_keep():
                keep[...] = block

            def early():
                choose((slot & bit) == bit, into_send, into_keep)

            choose(slot == (late ^ bit), into_rest, early)

        place(part[:rows], 1, send_a, keep_a, rest_a)
        place(part[rows:], 2, send_b, keep_b, rest_b)

    early_planes(*unit_refs, body)


def weight_late_kernel(group, *refs):
    inner_ref, outer_ref, own_ref, other_ref, rest_a, rest_b, send_a, send_b, keep_a, keep_b = refs
    rows = rest_a.shape[0]
    late = late_slot(group)

    def body(plane, unit_ref):
        part = weight_part(unit_ref, own_ref, other_ref)

        def place(block, bit, send, keep, rest):
            sends = (late & bit) == bit
            send[...] = jnp.where(sends, block, rest[...]).astype(BF16)
            keep[...] = jnp.where(sends, rest[...], block)

        place(part[:rows], 1, send_a, keep_a, rest_a)
        place(part[rows:], 2, send_b, keep_b, rest_b)

    late_plane(inner_ref, outer_ref, body)


def half_sum_kernel(group, *refs):
    late = late_slot(group)
    send_a, send_b, left_a, left_b = refs[8:]
    for stream, send, left, keeps in ((0, send_a, left_a, 2), (1, send_b, left_b, 1)):
        early_keep, early_from, late_keep, late_from = refs[4 * stream : 4 * stream + 4]
        early_sum = early_keep[...] + early_from[...].astype(F32)
        late_sum = late_keep[...] + late_from[...].astype(F32)
        goes = (late & keeps) == keeps
        send[...] = jnp.where(goes, late_sum, early_sum).astype(BF16)
        left[...] = jnp.where(goes, early_sum, late_sum)


def grad_sum_kernel(scale, left_a, left_b, from_a, from_b, out_ref):
    rows = left_a.shape[0]
    out_ref[:rows] = (left_a[...] + from_a[...].astype(F32)) * scale
    out_ref[rows:] = (left_b[...] + from_b[...].astype(F32)) * scale


def solution(mesh):
    blk, planes = mesh.shape["blk"], mesh.shape["shard"]
    assert planes == 4
    chips = blk // 2
    strips = chips // planes
    group = 2 * strips

    def swap(value, bit):
        return lax.ppermute(value, "blk", [(i, i ^ bit) for i in range(blk)])

    def pair_swap(value):
        return lax.ppermute(value, "shard", [(0, 1), (1, 0), (2, 3), (3, 2)])

    def mid_swap(value):
        pairs = []
        for b in range(blk):
            pairs += [(b * planes + z, b * planes + (3 - z)) for z in (1, 2)]
            pairs += [(b * planes + z, (b ^ 1) * planes + z) for z in (0, 3)]
        return lax.ppermute(value, ("blk", "shard"), pairs)

    def bound(kernel, *static):
        return lambda *refs: kernel(*static, *refs)

    def per_device(queries, key_rows, values, segment_ids, residual, out_weight, cotangent):
        count, width = queries.shape
        half = width // 2
        cut = half // 2
        position = lax.axis_index("blk") // 2
        unit_flops = 4 * half * count * width
        message = shape(half, 2 * count)

        cot_other = swap(cotangent, 1)

        w_own = out_weight.T
        bit = 1
        while bit < strips:
            there = swap(w_own, 2 * bit)
            upper = (position // bit) % 2
            w_own = jnp.concatenate(
                [jnp.where(upper, there, w_own), jnp.where(upper, w_own, there)], axis=0
            )
            bit *= 2
        w_one, w_two = swap(w_own, group), swap(w_own, 2 * group)
        unit = make_unit(cotangent, cot_other, strips)
        near, inner_far = pair_swap(unit), mid_swap(unit)
        ctx, probs = call(
            forward_kernel,
            (shape(count, width), shape(width // HEAD, count, count, dtype=F32)),
            queries,
            key_rows,
            values,
            segment_ids,
            flops=4 * count * count * width,
        )
        ctx_other = swap(ctx, 1)
        near, inner_far, w_one, w_two, ctx = lax.optimization_barrier(
            (near, inner_far, w_one, w_two, ctx)
        )
        w_far = [swap(w_two[:cut], group), swap(w_one[cut:], 2 * group)]
        w_all = jnp.stack([w_own, w_one, w_two, jnp.concatenate(w_far, axis=0)])

        outer_next, inner_next = pair_swap(inner_far), mid_swap(near)
        outer_next, inner_next = lax.optimization_barrier((outer_next, inner_next))
        early = call(
            bound(d_context_early_kernel, group),
            (shape(2 * count, width, dtype=F32),),
            unit,
            near,
            outer_next,
            inner_next,
            w_all,
            flops=3 * unit_flops,
        )[0]

        sources = (w_all, ctx, ctx_other)
        out = call(
            bound(first_message_kernel, group), (message,), *sources, inner_next, flops=unit_flops
        )[0]
        block, rest = shape(cut, width), shape(cut, width, dtype=F32)
        early_send_a, early_send_b, early_keep_a, early_keep_b, rest_a, rest_b = call(
            bound(weight_early_kernel, group),
            (block, block, rest, rest, rest, rest),
            unit,
            near,
            outer_next,
            inner_next,
            ctx,
            ctx_other,
            flops=3 * unit_flops,
        )
        early_from_a, early_from_b = swap(early_send_a, group), swap(early_send_b, 2 * group)
        passed, early, rest_a = lax.optimization_barrier((pair_swap(out), early, rest_a))
        late_send_a, late_send_b, late_keep_a, late_keep_b = call(
            bound(weight_late_kernel, group),
            (block, block, rest, rest),
            inner_far,
            passed,
            ctx,
            ctx_other,
            rest_a,
            rest_b,
            flops=unit_flops,
        )
        late_from_a, late_from_b = swap(late_send_a, group), swap(late_send_b, 2 * group)
        out = call(
            bound(message_kernel, 2, group), (message,), *sources, passed, flops=unit_flops
        )[0]
        from_pair, from_mid = pair_swap(out), mid_swap(out)
        early, late_send_a = lax.optimization_barrier((early, late_send_a))
        mine, send = call(
            bound(d_context_late_kernel, group),
            (shape(count, width, dtype=F32), shape(count, width)),
            inner_far,
            passed,
            w_all,
            early,
            flops=unit_flops,
        )
        d_queries, d_keys, d_values = call(
            backward_kernel,
            (shape(count, width),) * 3,
            queries,
            key_rows,
            values,
            probs,
            mine,
            swap(send, 1),
            flops=10 * count * count * width,
        )
        to_pair = call(
            bound(message_kernel, 1, group), (message,), *sources, from_mid, flops=unit_flops
        )[0]
        to_mid = call(
            bound(message_kernel, 3, group), (message,), *sources, from_pair, flops=unit_flops
        )[0]
        send_a, send_b, left_a, left_b = call(
            bound(half_sum_kernel, group),
            (block, block, rest, rest),
            early_keep_a,
            early_from_a,
            late_keep_a,
            late_from_a,
            early_keep_b,
            early_from_b,
            late_keep_b,
            late_from_b,
        )
        from_a, from_b = swap(send_a, 2 * group), swap(send_b, group)
        total = call(
            bound(grad_sum_kernel, 1.0 / math.sqrt(count * blk)),
            (shape(half, width, dtype=F32),),
            left_a,
            left_b,
            from_a,
            from_b,
        )[0]
        bit = strips // 2
        while bit >= 1:
            lower, upper = jnp.split(total, 2, axis=0)
            right = (position // bit) % 2
            sent = jnp.where(right, lower, upper)
            total = jnp.where(right, upper, lower) + swap(sent, 2 * bit)
            bit //= 2

        from_pair, from_mid, d_queries, total = lax.optimization_barrier(
            (pair_swap(to_pair), mid_swap(to_mid), d_queries, total)
        )
        keep, send = call(
            bound(last_project_kernel, group),
            (shape(half, count, dtype=F32),) * 2,
            *sources,
            from_pair,
            from_mid,
            flops=unit_flops,
        )
        layer_out = make_layer_out(residual, keep, swap(send, 1), strips)

        return layer_out, total, d_queries, d_keys, d_values

    spread = P("blk", "shard")
    return jax.shard_map(
        per_device,
        mesh=mesh,
        in_specs=(spread, spread, spread, P("blk", None), spread, P("shard", "blk"), spread),
        out_specs=(spread,) * 5,
        check_vma=False,
    )
```

```python
import math

import jax
import jax.numpy as jnp
from jax import lax
from jax.experimental import pallas as pl
from jax.experimental.pallas import tpu as pltpu
from jax.sharding import PartitionSpec as P

HEAD = 128
MASKED = -1e30
F32 = jnp.float32
BF16 = jnp.bfloat16
NT = (((1,), (1,)), ((), ()))
NN = (((1,), (0,)), ((), ()))
TN = (((0,), (0,)), ((), ()))


def dot(a, b, dims):
    return lax.dot_general(a, b, dims, preferred_element_type=F32)


def call(kernel, outs, *args, flops=0):
    size = sum(math.prod(o.shape) * o.dtype.itemsize for o in (*outs, *args))
    return pl.pallas_call(
        kernel,
        out_shape=tuple(outs),
        in_specs=[pl.BlockSpec(memory_space=pltpu.VMEM)] * len(args),
        out_specs=tuple([pl.BlockSpec(memory_space=pltpu.VMEM)] * len(outs)),
        compiler_params=pltpu.CompilerParams(vmem_limit_bytes=40 * 1024 * 1024),
        cost_estimate=pl.CostEstimate(flops=flops, bytes_accessed=size, transcendentals=0),
    )(*args)


def shape(*dims, dtype=BF16):
    return jax.ShapeDtypeStruct(dims, dtype)


def visible_mask(seg_ref):
    count = seg_ref.shape[1]
    seg = jnp.broadcast_to(seg_ref[...].astype(F32), (count, count))
    rows = lax.broadcasted_iota(jnp.int32, (count, count), 0)
    cols = lax.broadcasted_iota(jnp.int32, (count, count), 1)
    return (cols <= rows) & (seg == seg.T)


def head_probs(q, k, allowed):
    scores = dot(q, k, NT) * (1.0 / math.sqrt(HEAD))
    scores = jnp.where(allowed, scores, MASKED)
    weights = jnp.exp(scores - jnp.max(scores, axis=-1, keepdims=True))
    return weights / jnp.sum(weights, axis=-1, keepdims=True)


def forward_kernel(q_ref, k_ref, v_ref, seg_ref, ctx_ref, probs_ref):
    allowed = visible_mask(seg_ref)
    for h in range(q_ref.shape[1] // HEAD):
        at = pl.ds(h * HEAD, HEAD)
        probs = head_probs(q_ref[:, at], k_ref[:, at], allowed)
        probs_ref[h] = probs
        ctx_ref[:, at] = dot(probs.astype(BF16), v_ref[:, at], NN).astype(BF16)


def backward_kernel(q_ref, k_ref, v_ref, probs_ref, mine_ref, other_ref, dq_ref, dk_ref, dv_ref):
    scale = 1.0 / math.sqrt(HEAD)
    for h in range(q_ref.shape[1] // HEAD):
        at = pl.ds(h * HEAD, HEAD)
        q, k, v = q_ref[:, at], k_ref[:, at], v_ref[:, at]
        probs = probs_ref[h]
        d_ctx = (mine_ref[:, at] + other_ref[:, at].astype(F32)).astype(BF16)
        d_probs = dot(d_ctx, v, NT)
        dv_ref[:, at] = dot(probs.astype(BF16), d_ctx, TN).astype(BF16)
        inner = jnp.sum(probs * d_probs, axis=-1, keepdims=True)
        d_scores = (probs * (d_probs - inner)).astype(BF16)
        dq_ref[:, at] = (dot(d_scores, k, NN) * scale).astype(BF16)
        dk_ref[:, at] = (dot(d_scores, q, TN) * scale).astype(BF16)


def plane_slot(plane, group):
    return plane ^ (lax.axis_index("blk") // group)


def unit_kernel(own_ref, other_ref, unit_ref):
    half, count = unit_ref.shape[0], own_ref.shape[0]
    core = lax.rem(lax.axis_index("blk"), 2)
    own, other = own_ref[...].T, other_ref[...].T
    for side in range(2):

        @pl.when(core == side)
        def _():
            rows = slice(side * half, (side + 1) * half)
            unit_ref[:, :count] = own[rows]
            unit_ref[:, count:] = other[rows]


def make_unit(own, other, strips):
    count, width = own.shape
    half = width // 2
    if strips == 1:
        return call(unit_kernel, (shape(half, 2 * count),), own, other)[0]
    core = lax.rem(lax.axis_index("blk"), 2)
    both = jnp.concatenate([own, other], axis=0).T.reshape(strips, 2, half // strips, 2 * count)
    return lax.dynamic_index_in_dim(both, core, 1, keepdims=False).reshape(half, 2 * count)


def is_inner(z):
    return (z == 1) | (z == 2)


def own_bits():
    core = lax.rem(lax.axis_index("blk"), 2)
    return 1 + core, 2 - core


def late_slot(group):
    return plane_slot(lax.axis_index("shard") ^ 3, group)


def project_part(w_ref, ctx_ref, plane, group):
    return dot(w_ref[plane_slot(plane, group)], ctx_ref[...], NT)


def choose(condition, then, other):
    pl.when(condition)(then)
    pl.when(~condition)(other)


def first_message_kernel(group, own_w, near_w, soon_w, own_ref, other_ref, passing_ref, out_ref):
    count = own_ref.shape[0]
    z, slot, first = lax.axis_index("shard"), late_slot(group), own_bits()[0]

    def share(w_ref):
        for i, ctx_ref in enumerate((own_ref, other_ref)):
            out_ref[:, pl.ds(i * count, count)] = dot(w_ref[...], ctx_ref[...], NT).astype(BF16)

    @pl.when(is_inner(z))
    def _():
        out_ref[...] = passing_ref[...]

    for place, w_ref in (
        (slot == 0, own_w),
        (slot == first, near_w),
        ((slot != 0) & (slot != first), soon_w),
    ):
        pl.when(~is_inner(z) & place)(lambda w_ref=w_ref: share(w_ref))


def all_columns_kernel(group, own_w, near_w, soon_w, last_w, out_ref):
    first, second = own_bits()
    out_ref[0] = own_w[...]
    out_ref[first] = near_w[...]
    far_soon = (late_slot(group) & first) == first
    out_ref[jnp.where(far_soon, 3, second)] = soon_w[...]
    out_ref[jnp.where(far_soon, second, 3)] = last_w[...]


def second_message_kernel(group, w_ref, own_ref, other_ref, passing_ref, out_ref):
    count = own_ref.shape[0]
    z = lax.axis_index("shard")

    @pl.when(is_inner(z))
    def _():
        out_ref[...] = passing_ref[...]

    @pl.when(~is_inner(z))
    def _():
        for i, ctx_ref in enumerate((own_ref, other_ref)):
            part = project_part(w_ref, ctx_ref, z ^ 2, group)
            out_ref[:, pl.ds(i * count, count)] = part.astype(BF16)


def message_kernel(flip, group, w_ref, own_ref, other_ref, past_ref, out_ref):
    count = own_ref.shape[0]
    z = lax.axis_index("shard")
    for i, ctx_ref in enumerate((own_ref, other_ref)):
        at = pl.ds(i * count, count)
        part = project_part(w_ref, ctx_ref, z ^ flip, group)
        past = jnp.where(is_inner(z), past_ref[:, at].astype(F32), 0.0)
        out_ref[:, at] = (part + past).astype(BF16)


def last_project_kernel(group, w_ref, own_ref, other_ref, pair_ref, mid_ref, keep_ref, send_ref):
    count = own_ref.shape[0]
    z = lax.axis_index("shard")
    for i, (ctx_ref, out_ref) in enumerate(((own_ref, keep_ref), (other_ref, send_ref))):
        at = pl.ds(i * count, count)
        part = project_part(w_ref, ctx_ref, z, group) + pair_ref[:, at].astype(F32)
        out_ref[...] = part + jnp.where(is_inner(z), mid_ref[:, at].astype(F32), 0.0)


def layer_out_kernel(residual_ref, keep_ref, other_ref, out_ref):
    half = keep_ref.shape[0]
    core = lax.rem(lax.axis_index("blk"), 2)
    keep, other = keep_ref[...], other_ref[...]
    for side, order in enumerate(((keep, other), (other, keep))):

        @pl.when(core == side)
        def _():
            total = jnp.concatenate(order, axis=0).T
            out_ref[...] = (residual_ref[...].astype(F32) + total).astype(BF16)


def make_layer_out(residual, keep, other, strips):
    count, width = residual.shape
    if strips == 1:
        return call(layer_out_kernel, (shape(count, width),), residual, keep, other)[0]
    core = lax.rem(lax.axis_index("blk"), 2)
    pair = jnp.stack([keep, other]).reshape(2, strips, -1, count)
    pair = jnp.where(core == 0, pair, pair[::-1])
    total = pair.transpose(1, 0, 2, 3).reshape(width, count)
    return (residual.astype(F32) + total.T).astype(BF16)


def early_planes(unit_ref, near_ref, outer_ref, inner_ref, body):
    z = lax.axis_index("shard")
    body(z, unit_ref)
    body(z ^ 1, near_ref)
    pl.when(is_inner(z))(lambda: body(z ^ 2, inner_ref))
    pl.when(~is_inner(z))(lambda: body(z ^ 2, outer_ref))


def late_plane(inner_ref, outer_ref, body):
    z = lax.axis_index("shard")
    pl.when(is_inner(z))(lambda: body(z ^ 3, inner_ref))
    pl.when(~is_inner(z))(lambda: body(z ^ 3, outer_ref))


def d_context_early_kernel(group, *refs):
    *unit_refs, w_ref, total_ref = refs
    total_ref[...] = jnp.zeros_like(total_ref)

    def body(plane, unit_ref):
        total_ref[...] += dot(unit_ref[...], w_ref[plane_slot(plane, group)], TN)

    early_planes(*unit_refs, body)


def d_context_late_kernel(group, *refs):
    inner_ref, outer_ref, w_ref, total_ref, mine_ref, send_ref = refs
    count = mine_ref.shape[0]

    def body(plane, unit_ref):
        part = dot(unit_ref[...], w_ref[plane_slot(plane, group)], TN)
        mine_ref[...] = total_ref[:count] + part[:count]
        send_ref[...] = (total_ref[count:] + part[count:]).astype(BF16)

    late_plane(inner_ref, outer_ref, body)


def weight_part(unit_ref, own_ref, other_ref):
    count = own_ref.shape[0]
    part = dot(unit_ref[:, :count], own_ref[...], NN)
    return part + dot(unit_ref[:, count:], other_ref[...], NN)


def weight_early_kernel(group, *refs):
    *unit_refs, own_ref, other_ref, send, keep, rest = refs
    late, first = late_slot(group), own_bits()[0]

    def body(plane, unit_ref):
        slot = plane_slot(plane, group)
        part = weight_part(unit_ref, own_ref, other_ref)

        def into_rest():
            rest[...] = part

        def into_send():
            send[...] = part.astype(BF16)

        def into_keep():
            keep[...] = part

        def early():
            choose((slot & first) == first, into_send, into_keep)

        choose(slot == (late ^ first), into_rest, early)

    early_planes(*unit_refs, body)


def weight_late_kernel(group, inner_ref, outer_ref, own_ref, other_ref, rest, send, keep):
    late, first = late_slot(group), own_bits()[0]
    sends = (late & first) == first

    def body(plane, unit_ref):
        part = weight_part(unit_ref, own_ref, other_ref)
        send[...] = jnp.where(sends, part, rest[...]).astype(BF16)
        keep[...] = jnp.where(sends, rest[...], part)

    late_plane(inner_ref, outer_ref, body)


def half_sum_kernel(group, early_keep, early_from, late_keep, late_from, send, left):
    second = own_bits()[1]
    goes = (late_slot(group) & second) == second
    early_sum = early_keep[...] + early_from[...].astype(F32)
    late_sum = late_keep[...] + late_from[...].astype(F32)
    send[...] = jnp.where(goes, late_sum, early_sum).astype(BF16)
    left[...] = jnp.where(goes, early_sum, late_sum)


def grad_sum_kernel(scale, left_ref, from_ref, out_ref):
    out_ref[...] = (left_ref[...] + from_ref[...].astype(F32)) * scale


def solution(mesh):
    blk, planes = mesh.shape["blk"], mesh.shape["shard"]
    assert planes == 4
    chips = blk // 2
    strips = chips // planes
    group = 2 * strips

    def swap(value, bit):
        return lax.ppermute(value, "blk", [(i, i ^ bit) for i in range(blk)])

    def core_swap(value, first):
        bits = (1, 2) if first else (2, 1)
        return lax.ppermute(value, "blk", [(i, i ^ (group * bits[i % 2])) for i in range(blk)])

    def pair_swap(value):
        return lax.ppermute(value, "shard", [(0, 1), (1, 0), (2, 3), (3, 2)])

    def mid_swap(value):
        pairs = []
        for b in range(blk):
            pairs += [(b * planes + z, b * planes + (3 - z)) for z in (1, 2)]
            pairs += [(b * planes + z, (b ^ 1) * planes + z) for z in (0, 3)]
        return lax.ppermute(value, ("blk", "shard"), pairs)

    def together(*values):
        return lax.optimization_barrier(values)

    def bound(kernel, *static):
        return lambda *refs: kernel(*static, *refs)

    def per_device(queries, key_rows, values, segment_ids, residual, out_weight, cotangent):
        count, width = queries.shape
        half = width // 2
        position = lax.axis_index("blk") // 2
        unit_flops = 4 * half * count * width
        message = shape(half, 2 * count)

        cot_other = swap(cotangent, 1)

        w_own = out_weight.T
        bit = 1
        while bit < strips:
            there = swap(w_own, 2 * bit)
            upper = (position // bit) % 2
            w_own = jnp.concatenate(
                [jnp.where(upper, there, w_own), jnp.where(upper, w_own, there)], axis=0
            )
            bit *= 2

        w_near = core_swap(w_own, True)
        unit = make_unit(cotangent, cot_other, strips)
        near, inner_far = pair_swap(unit), mid_swap(unit)

        first = own_bits()[0]
        far_soon = (late_slot(group) & first) == first
        w_soon = core_swap(jnp.where(far_soon, w_near, w_own), False)
        w_last = core_swap(jnp.where(far_soon, w_own, w_near), False)
        asked, w_near = together(queries, w_near)
        ctx, probs = call(
            forward_kernel,
            (shape(count, width), shape(width // HEAD, count, count, dtype=F32)),
            asked,
            key_rows,
            values,
            segment_ids,
            flops=4 * count * count * width,
        )
        near, inner_far, ctx = together(near, inner_far, ctx)
        ctx_other = swap(ctx, 1)

        inner_next = mid_swap(near)
        out = call(
            bound(first_message_kernel, group),
            (message,),
            w_own,
            w_near,
            w_soon,
            ctx,
            ctx_other,
            inner_far,
            flops=unit_flops,
        )[0]
        pair_two = pair_swap(out)
        w_all = call(
            bound(all_columns_kernel, group),
            (shape(planes, half, width),),
            w_own,
            w_near,
            w_soon,
            w_last,
        )[0]
        sources = (w_all, ctx, ctx_other)

        out = call(
            bound(second_message_kernel, group), (message,), *sources, inner_next, flops=unit_flops
        )[0]
        pair_three = pair_swap(out)
        out, pair_two = together(out, pair_two)
        out = call(
            bound(message_kernel, 2, group), (message,), *sources, pair_two, flops=unit_flops
        )[0]
        mid_three = mid_swap(out)
        block, rest = shape(half, width), shape(half, width, dtype=F32)
        ready = (unit, near, pair_two, inner_next)
        early_send, early_keep, early_rest = call(
            bound(weight_early_kernel, group),
            (block, rest, rest),
            *ready,
            ctx,
            ctx_other,
            flops=3 * unit_flops,
        )
        early_from = core_swap(early_send, True)
        d_ctx_early = call(
            bound(d_context_early_kernel, group),
            (shape(2 * count, width, dtype=F32),),
            *ready,
            w_all,
            flops=3 * unit_flops,
        )[0]
        pair_three, d_ctx_early, early_rest = together(pair_three, d_ctx_early, early_rest)

        late_send, late_keep = call(
            bound(weight_late_kernel, group),
            (block, rest),
            inner_far,
            pair_three,
            ctx,
            ctx_other,
            early_rest,
            flops=unit_flops,
        )
        late_from = core_swap(late_send, True)
        d_ctx_early, late_send = together(d_ctx_early, late_send)
        mine, send = call(
            bound(d_context_late_kernel, group),
            (shape(count, width, dtype=F32), shape(count, width)),
            inner_far,
            pair_three,
            w_all,
            d_ctx_early,
            flops=unit_flops,
        )
        d_ctx_other = swap(send, 1)
        mine, pair_three, early_from = together(mine, pair_three, early_from)
        out = call(
            bound(message_kernel, 3, group), (message,), *sources, pair_three, flops=unit_flops
        )[0]
        mid_four = mid_swap(out)
        out = call(
            bound(message_kernel, 1, group), (message,), *sources, mid_three, flops=unit_flops
        )[0]
        pair_four = pair_swap(out)
        late_from, out = together(late_from, out)
        send, left = call(
            bound(half_sum_kernel, group), (block, rest), early_keep, early_from, late_keep, late_from
        )
        second_from = core_swap(send, False)

        mine, send = together(mine, send)
        d_queries, d_keys, d_values = call(
            backward_kernel,
            (shape(count, width),) * 3,
            queries,
            key_rows,
            values,
            probs,
            mine,
            d_ctx_other,
            flops=10 * count * count * width,
        )
        pair_four, mid_four, d_queries = together(pair_four, mid_four, d_queries)
        keep, send = call(
            bound(last_project_kernel, group),
            (shape(half, count, dtype=F32),) * 2,
            *sources,
            pair_four,
            mid_four,
            flops=unit_flops,
        )
        last_other = swap(send, 1)
        left, keep = together(left, keep)
        total = call(
            bound(grad_sum_kernel, 1.0 / math.sqrt(count * blk)),
            (shape(half, width, dtype=F32),),
            left,
            second_from,
        )[0]
        layer_out = make_layer_out(residual, keep, last_other, strips)
        bit = strips // 2
        while bit >= 1:
            lower, upper = jnp.split(total, 2, axis=0)
            right = (position // bit) % 2
            sent = jnp.where(right, lower, upper)
            total = jnp.where(right, upper, lower) + swap(sent, 2 * bit)
            bit //= 2

        return layer_out, total, d_queries, d_keys, d_values

    spread = P("blk", "shard")
    return jax.shard_map(
        per_device,
        mesh=mesh,
        in_specs=(spread, spread, spread, P("blk", None), spread, P("shard", "blk"), spread),
        out_specs=(spread,) * 5,
        check_vma=False,
    )
```

```python
import math

import jax
import jax.numpy as jnp
from jax import lax
from jax.experimental import pallas as pl
from jax.experimental.pallas import tpu as pltpu
from jax.sharding import PartitionSpec as P

HEAD = 128
MASKED = -1e30
F32 = jnp.float32
BF16 = jnp.bfloat16
NT = (((1,), (1,)), ((), ()))
NN = (((1,), (0,)), ((), ()))
TN = (((0,), (0,)), ((), ()))


def dot(a, b, dims):
    return lax.dot_general(a, b, dims, preferred_element_type=F32)


def call(kernel, outs, *args, flops=0):
    size = sum(math.prod(o.shape) * o.dtype.itemsize for o in (*outs, *args))
    return pl.pallas_call(
        kernel,
        out_shape=tuple(outs),
        in_specs=[pl.BlockSpec(memory_space=pltpu.VMEM)] * len(args),
        out_specs=tuple([pl.BlockSpec(memory_space=pltpu.VMEM)] * len(outs)),
        compiler_params=pltpu.CompilerParams(vmem_limit_bytes=40 * 1024 * 1024),
        cost_estimate=pl.CostEstimate(flops=flops, bytes_accessed=size, transcendentals=0),
    )(*args)


def shape(*dims, dtype=BF16):
    return jax.ShapeDtypeStruct(dims, dtype)


def visible_mask(seg_ref):
    count = seg_ref.shape[1]
    seg = jnp.broadcast_to(seg_ref[...].astype(F32), (count, count))
    rows = lax.broadcasted_iota(jnp.int32, (count, count), 0)
    cols = lax.broadcasted_iota(jnp.int32, (count, count), 1)
    return (cols <= rows) & (seg == seg.T)


def head_probs(q, k, allowed):
    scores = dot(q, k, NT) * (1.0 / math.sqrt(HEAD))
    scores = jnp.where(allowed, scores, MASKED)
    weights = jnp.exp(scores - jnp.max(scores, axis=-1, keepdims=True))
    return weights / jnp.sum(weights, axis=-1, keepdims=True)


def forward_kernel(q_ref, k_ref, v_ref, seg_ref, ctx_ref, probs_ref):
    allowed = visible_mask(seg_ref)
    for h in range(q_ref.shape[1] // HEAD):
        at = pl.ds(h * HEAD, HEAD)
        probs = head_probs(q_ref[:, at], k_ref[:, at], allowed)
        probs_ref[h] = probs
        ctx_ref[:, at] = dot(probs.astype(BF16), v_ref[:, at], NN).astype(BF16)


def backward_kernel(q_ref, k_ref, v_ref, probs_ref, mine_ref, other_ref, dq_ref, dk_ref, dv_ref):
    scale = 1.0 / math.sqrt(HEAD)
    for h in range(q_ref.shape[1] // HEAD):
        at = pl.ds(h * HEAD, HEAD)
        q, k, v = q_ref[:, at], k_ref[:, at], v_ref[:, at]
        probs = probs_ref[h]
        d_ctx = (mine_ref[:, at] + other_ref[:, at].astype(F32)).astype(BF16)
        d_probs = dot(d_ctx, v, NT)
        dv_ref[:, at] = dot(probs.astype(BF16), d_ctx, TN).astype(BF16)
        inner = jnp.sum(probs * d_probs, axis=-1, keepdims=True)
        d_scores = (probs * (d_probs - inner)).astype(BF16)
        dq_ref[:, at] = (dot(d_scores, k, NN) * scale).astype(BF16)
        dk_ref[:, at] = (dot(d_scores, q, TN) * scale).astype(BF16)


def plane_slot(plane, group):
    return plane ^ (lax.axis_index("blk") // group)


def unit_kernel(own_ref, other_ref, unit_ref):
    half, count = unit_ref.shape[0], own_ref.shape[0]
    core = lax.rem(lax.axis_index("blk"), 2)
    own, other = own_ref[...].T, other_ref[...].T
    for side in range(2):

        @pl.when(core == side)
        def _():
            rows = slice(side * half, (side + 1) * half)
            unit_ref[:, :count] = own[rows]
            unit_ref[:, count:] = other[rows]


def make_unit(own, other, strips):
    count, width = own.shape
    half = width // 2
    if strips == 1:
        return call(unit_kernel, (shape(half, 2 * count),), own, other)[0]
    core = lax.rem(lax.axis_index("blk"), 2)
    both = jnp.concatenate([own, other], axis=0).T.reshape(strips, 2, half // strips, 2 * count)
    return lax.dynamic_index_in_dim(both, core, 1, keepdims=False).reshape(half, 2 * count)


def is_inner(z):
    return (z == 1) | (z == 2)


def own_bits():
    core = lax.rem(lax.axis_index("blk"), 2)
    return 1 + core, 2 - core


def late_slot(group):
    return plane_slot(lax.axis_index("shard") ^ 3, group)


def project_part(w_ref, ctx_ref, plane, group):
    return dot(w_ref[plane_slot(plane, group)], ctx_ref[...], NT)


def choose(condition, then, other):
    pl.when(condition)(then)
    pl.when(~condition)(other)


def first_message_kernel(group, own_w, near_w, soon_w, own_ref, other_ref, passing_ref, out_ref):
    count = own_ref.shape[0]
    z, slot, first = lax.axis_index("shard"), late_slot(group), own_bits()[0]

    def share(w_ref):
        for i, ctx_ref in enumerate((own_ref, other_ref)):
            out_ref[:, pl.ds(i * count, count)] = dot(w_ref[...], ctx_ref[...], NT).astype(BF16)

    @pl.when(is_inner(z))
    def _():
        out_ref[...] = passing_ref[...]

    for place, w_ref in (
        (slot == 0, own_w),
        (slot == first, near_w),
        ((slot != 0) & (slot != first), soon_w),
    ):
        pl.when(~is_inner(z) & place)(lambda w_ref=w_ref: share(w_ref))


def all_columns_kernel(group, own_w, near_w, soon_w, last_w, out_ref):
    first, second = own_bits()
    out_ref[0] = own_w[...]
    out_ref[first] = near_w[...]
    far_soon = (late_slot(group) & first) == first
    out_ref[jnp.where(far_soon, 3, second)] = soon_w[...]
    out_ref[jnp.where(far_soon, second, 3)] = last_w[...]


def second_message_kernel(group, w_ref, own_ref, other_ref, passing_ref, out_ref):
    count = own_ref.shape[0]
    z = lax.axis_index("shard")

    @pl.when(is_inner(z))
    def _():
        out_ref[...] = passing_ref[...]

    @pl.when(~is_inner(z))
    def _():
        for i, ctx_ref in enumerate((own_ref, other_ref)):
            part = project_part(w_ref, ctx_ref, z ^ 2, group)
            out_ref[:, pl.ds(i * count, count)] = part.astype(BF16)


def message_kernel(flip, group, w_ref, own_ref, other_ref, past_ref, out_ref):
    count = own_ref.shape[0]
    z = lax.axis_index("shard")
    for i, ctx_ref in enumerate((own_ref, other_ref)):
        at = pl.ds(i * count, count)
        part = project_part(w_ref, ctx_ref, z ^ flip, group)
        past = jnp.where(is_inner(z), past_ref[:, at].astype(F32), 0.0)
        out_ref[:, at] = (part + past).astype(BF16)


def last_project_kernel(group, w_ref, own_ref, other_ref, pair_ref, mid_ref, keep_ref, send_ref):
    count = own_ref.shape[0]
    z = lax.axis_index("shard")
    for i, (ctx_ref, out_ref) in enumerate(((own_ref, keep_ref), (other_ref, send_ref))):
        at = pl.ds(i * count, count)
        part = project_part(w_ref, ctx_ref, z, group) + pair_ref[:, at].astype(F32)
        out_ref[...] = part + jnp.where(is_inner(z), mid_ref[:, at].astype(F32), 0.0)


def layer_out_kernel(residual_ref, keep_ref, other_ref, out_ref):
    half = keep_ref.shape[0]
    core = lax.rem(lax.axis_index("blk"), 2)
    keep, other = keep_ref[...], other_ref[...]
    for side, order in enumerate(((keep, other), (other, keep))):

        @pl.when(core == side)
        def _():
            total = jnp.concatenate(order, axis=0).T
            out_ref[...] = (residual_ref[...].astype(F32) + total).astype(BF16)


def make_layer_out(residual, keep, other, strips):
    count, width = residual.shape
    if strips == 1:
        return call(layer_out_kernel, (shape(count, width),), residual, keep, other)[0]
    core = lax.rem(lax.axis_index("blk"), 2)
    pair = jnp.stack([keep, other]).reshape(2, strips, -1, count)
    pair = jnp.where(core == 0, pair, pair[::-1])
    total = pair.transpose(1, 0, 2, 3).reshape(width, count)
    return (residual.astype(F32) + total.T).astype(BF16)


def early_planes(unit_ref, near_ref, outer_ref, inner_ref, body):
    z = lax.axis_index("shard")
    body(z, unit_ref)
    body(z ^ 1, near_ref)
    pl.when(is_inner(z))(lambda: body(z ^ 2, inner_ref))
    pl.when(~is_inner(z))(lambda: body(z ^ 2, outer_ref))


def late_plane(inner_ref, outer_ref, body):
    z = lax.axis_index("shard")
    pl.when(is_inner(z))(lambda: body(z ^ 3, inner_ref))
    pl.when(~is_inner(z))(lambda: body(z ^ 3, outer_ref))


def d_context_early_kernel(group, *refs):
    *unit_refs, w_ref, total_ref = refs
    total_ref[...] = jnp.zeros_like(total_ref)

    def body(plane, unit_ref):
        total_ref[...] += dot(unit_ref[...], w_ref[plane_slot(plane, group)], TN)

    early_planes(*unit_refs, body)


def d_context_late_kernel(group, *refs):
    inner_ref, outer_ref, w_ref, total_ref, mine_ref, send_ref = refs
    count = mine_ref.shape[0]

    def body(plane, unit_ref):
        part = dot(unit_ref[...], w_ref[plane_slot(plane, group)], TN)
        mine_ref[...] = total_ref[:count] + part[:count]
        send_ref[...] = (total_ref[count:] + part[count:]).astype(BF16)

    late_plane(inner_ref, outer_ref, body)


def weight_part(unit_ref, own_ref, other_ref):
    count = own_ref.shape[0]
    part = dot(unit_ref[:, :count], own_ref[...], NN)
    return part + dot(unit_ref[:, count:], other_ref[...], NN)


def weight_early_kernel(group, *refs):
    *unit_refs, own_ref, other_ref, send_a, send_b, keep, rest = refs
    rows = send_a.shape[0]
    late, first = late_slot(group), own_bits()[0]

    def body(plane, unit_ref):
        slot = plane_slot(plane, group)
        part = weight_part(unit_ref, own_ref, other_ref)

        def into_rest():
            rest[...] = part

        def into_send():
            send_a[...] = part[:rows].astype(BF16)
            send_b[...] = part[rows:].astype(BF16)

        def into_keep():
            keep[...] = part

        def early():
            choose((slot & first) == first, into_send, into_keep)

        choose(slot == (late ^ first), into_rest, early)

    early_planes(*unit_refs, body)


def weight_late_kernel(group, inner_ref, outer_ref, own_ref, other_ref, rest, send, keep):
    late, first = late_slot(group), own_bits()[0]
    sends = (late & first) == first

    def body(plane, unit_ref):
        part = weight_part(unit_ref, own_ref, other_ref)
        send[...] = jnp.where(sends, part, rest[...]).astype(BF16)
        keep[...] = jnp.where(sends, rest[...], part)

    late_plane(inner_ref, outer_ref, body)


def half_sum_kernel(group, early_keep, early_from_a, early_from_b, late_keep, late_from, send, left):
    rows = early_from_a.shape[0]
    second = own_bits()[1]
    goes = (late_slot(group) & second) == second
    for at, early_from in ((pl.ds(0, rows), early_from_a), (pl.ds(rows, rows), early_from_b)):
        early_sum = early_keep[at] + early_from[...].astype(F32)
        late_sum = late_keep[at] + late_from[at].astype(F32)
        send[at] = jnp.where(goes, late_sum, early_sum).astype(BF16)
        left[at] = jnp.where(goes, early_sum, late_sum)


def grad_sum_kernel(scale, left_ref, from_ref, out_ref):
    out_ref[...] = (left_ref[...] + from_ref[...].astype(F32)) * scale


def solution(mesh):
    blk, planes = mesh.shape["blk"], mesh.shape["shard"]
    assert planes == 4
    chips = blk // 2
    strips = chips // planes
    group = 2 * strips

    def swap(value, bit):
        return lax.ppermute(value, "blk", [(i, i ^ bit) for i in range(blk)])

    def core_swap(value, first):
        bits = (1, 2) if first else (2, 1)
        return lax.ppermute(value, "blk", [(i, i ^ (group * bits[i % 2])) for i in range(blk)])

    def pair_swap(value):
        return lax.ppermute(value, "shard", [(0, 1), (1, 0), (2, 3), (3, 2)])

    def mid_swap(value):
        pairs = []
        for b in range(blk):
            pairs += [(b * planes + z, b * planes + (3 - z)) for z in (1, 2)]
            pairs += [(b * planes + z, (b ^ 1) * planes + z) for z in (0, 3)]
        return lax.ppermute(value, ("blk", "shard"), pairs)

    def together(*values):
        return lax.optimization_barrier(values)

    def bound(kernel, *static):
        return lambda *refs: kernel(*static, *refs)

    def per_device(queries, key_rows, values, segment_ids, residual, out_weight, cotangent):
        count, width = queries.shape
        half = width // 2
        position = lax.axis_index("blk") // 2
        unit_flops = 4 * half * count * width
        message = shape(half, 2 * count)

        cot_other = swap(cotangent, 1)

        w_own = out_weight.T
        bit = 1
        while bit < strips:
            there = swap(w_own, 2 * bit)
            upper = (position // bit) % 2
            w_own = jnp.concatenate(
                [jnp.where(upper, there, w_own), jnp.where(upper, w_own, there)], axis=0
            )
            bit *= 2

        w_near = core_swap(w_own, True)
        unit = make_unit(cotangent, cot_other, strips)
        near, inner_far = pair_swap(unit), mid_swap(unit)

        first = own_bits()[0]
        far_soon = (late_slot(group) & first) == first
        w_soon = core_swap(jnp.where(far_soon, w_near, w_own), False)
        w_last = core_swap(jnp.where(far_soon, w_own, w_near), False)
        asked, w_near = together(queries, w_near)
        ctx, probs = call(
            forward_kernel,
            (shape(count, width), shape(width // HEAD, count, count, dtype=F32)),
            asked,
            key_rows,
            values,
            segment_ids,
            flops=4 * count * count * width,
        )
        near, inner_far, ctx = together(near, inner_far, ctx)
        ctx_other = swap(ctx, 1)

        inner_next = mid_swap(near)
        out = call(
            bound(first_message_kernel, group),
            (message,),
            w_own,
            w_near,
            w_soon,
            ctx,
            ctx_other,
            inner_far,
            flops=unit_flops,
        )[0]
        pair_two = pair_swap(out)
        w_all = call(
            bound(all_columns_kernel, group),
            (shape(planes, half, width),),
            w_own,
            w_near,
            w_soon,
            w_last,
        )[0]
        sources = (w_all, ctx, ctx_other)

        out = call(
            bound(second_message_kernel, group), (message,), *sources, inner_next, flops=unit_flops
        )[0]
        pair_three = pair_swap(out)
        out, pair_two = together(out, pair_two)
        out = call(
            bound(message_kernel, 2, group), (message,), *sources, pair_two, flops=unit_flops
        )[0]
        mid_three = mid_swap(out)
        block, rest = shape(half, width), shape(half, width, dtype=F32)
        ready = (unit, near, pair_two, inner_next)
        piece = shape(half // 2, width)
        early_send_a, early_send_b, early_keep, early_rest = call(
            bound(weight_early_kernel, group),
            (piece, piece, rest, rest),
            *ready,
            ctx,
            ctx_other,
            flops=3 * unit_flops,
        )
        early_from_a, early_from_b = core_swap(early_send_a, True), core_swap(early_send_b, True)
        d_ctx_early = call(
            bound(d_context_early_kernel, group),
            (shape(2 * count, width, dtype=F32),),
            *ready,
            w_all,
            flops=3 * unit_flops,
        )[0]
        pair_three, d_ctx_early, early_rest = together(pair_three, d_ctx_early, early_rest)

        late_send, late_keep = call(
            bound(weight_late_kernel, group),
            (block, rest),
            inner_far,
            pair_three,
            ctx,
            ctx_other,
            early_rest,
            flops=unit_flops,
        )
        late_from = core_swap(late_send, True)
        mid_three, late_send = together(mid_three, late_send)
        out = call(
            bound(message_kernel, 1, group), (message,), *sources, mid_three, flops=unit_flops
        )[0]
        pair_four = pair_swap(out)
        pair_three, early_from_a, early_from_b, out = together(pair_three, early_from_a, early_from_b, out)
        out = call(
            bound(message_kernel, 3, group), (message,), *sources, pair_three, flops=unit_flops
        )[0]
        mid_four = mid_swap(out)
        d_ctx_early, out = together(d_ctx_early, out)
        mine, send = call(
            bound(d_context_late_kernel, group),
            (shape(count, width, dtype=F32), shape(count, width)),
            inner_far,
            pair_three,
            w_all,
            d_ctx_early,
            flops=unit_flops,
        )
        d_ctx_other = swap(send, 1)
        late_from, out = together(late_from, out)
        send, left = call(
            bound(half_sum_kernel, group), (block, rest), early_keep, early_from_a, early_from_b, late_keep, late_from
        )
        second_from = core_swap(send, False)

        pair_four, mid_four = together(pair_four, mid_four)
        keep, send = call(
            bound(last_project_kernel, group),
            (shape(half, count, dtype=F32),) * 2,
            *sources,
            pair_four,
            mid_four,
            flops=unit_flops,
        )
        last_other = swap(send, 1)
        mine, keep = together(mine, keep)
        d_queries, d_keys, d_values = call(
            backward_kernel,
            (shape(count, width),) * 3,
            queries,
            key_rows,
            values,
            probs,
            mine,
            d_ctx_other,
            flops=10 * count * count * width,
        )
        layer_out = make_layer_out(residual, keep, last_other, strips)
        left, layer_out = together(left, layer_out)
        total = call(
            bound(grad_sum_kernel, 1.0 / math.sqrt(count * blk)),
            (shape(half, width, dtype=F32),),
            left,
            second_from,
        )[0]
        bit = strips // 2
        while bit >= 1:
            lower, upper = jnp.split(total, 2, axis=0)
            right = (position // bit) % 2
            sent = jnp.where(right, lower, upper)
            total = jnp.where(right, upper, lower) + swap(sent, 2 * bit)
            bit //= 2

        return layer_out, total, d_queries, d_keys, d_values

    spread = P("blk", "shard")
    return jax.shard_map(
        per_device,
        mesh=mesh,
        in_specs=(spread, spread, spread, P("blk", None), spread, P("shard", "blk"), spread),
        out_specs=(spread,) * 5,
        check_vma=False,
    )
```

```python
import math

import jax
import jax.numpy as jnp
from jax import lax
from jax.experimental import pallas as pl
from jax.experimental.pallas import tpu as pltpu
from jax.sharding import PartitionSpec as P

HEAD = 128
MASKED = -1e30
F32 = jnp.float32
BF16 = jnp.bfloat16
NT = (((1,), (1,)), ((), ()))
NN = (((1,), (0,)), ((), ()))
TN = (((0,), (0,)), ((), ()))


def dot(a, b, dims):
    return lax.dot_general(a, b, dims, preferred_element_type=F32)


def call(kernel, outs, *args, flops=0):
    size = sum(math.prod(o.shape) * o.dtype.itemsize for o in (*outs, *args))
    return pl.pallas_call(
        kernel,
        out_shape=tuple(outs),
        in_specs=[pl.BlockSpec(memory_space=pltpu.VMEM)] * len(args),
        out_specs=tuple([pl.BlockSpec(memory_space=pltpu.VMEM)] * len(outs)),
        compiler_params=pltpu.CompilerParams(vmem_limit_bytes=40 * 1024 * 1024),
        cost_estimate=pl.CostEstimate(flops=flops, bytes_accessed=size, transcendentals=0),
    )(*args)


def shape(*dims, dtype=BF16):
    return jax.ShapeDtypeStruct(dims, dtype)


def visible_mask(seg_ref):
    count = seg_ref.shape[1]
    seg = jnp.broadcast_to(seg_ref[...].astype(F32), (count, count))
    rows = lax.broadcasted_iota(jnp.int32, (count, count), 0)
    cols = lax.broadcasted_iota(jnp.int32, (count, count), 1)
    return (cols <= rows) & (seg == seg.T)


def head_probs(q, k, allowed):
    scores = dot(q, k, NT) * (1.0 / math.sqrt(HEAD))
    scores = jnp.where(allowed, scores, MASKED)
    weights = jnp.exp(scores - jnp.max(scores, axis=-1, keepdims=True))
    return weights / jnp.sum(weights, axis=-1, keepdims=True)


def forward_kernel(q_ref, k_ref, v_ref, seg_ref, ctx_ref, low_ref, high_ref, probs_ref):
    allowed = visible_mask(seg_ref)
    for h in range(q_ref.shape[1] // HEAD):
        at = pl.ds(h * HEAD, HEAD)
        probs = head_probs(q_ref[:, at], k_ref[:, at], allowed)
        probs_ref[h] = probs
        ctx = dot(probs.astype(BF16), v_ref[:, at], NN).astype(BF16)
        ctx_ref[:, at] = ctx
        low_ref[:, at], high_ref[:, at] = jnp.split(ctx, 2, axis=0)


def backward_kernel(q_ref, k_ref, v_ref, probs_ref, mine_ref, other_ref, dq_ref, dk_ref, dv_ref):
    scale = 1.0 / math.sqrt(HEAD)
    for h in range(q_ref.shape[1] // HEAD):
        at = pl.ds(h * HEAD, HEAD)
        q, k, v = q_ref[:, at], k_ref[:, at], v_ref[:, at]
        probs = probs_ref[h]
        d_ctx = (mine_ref[:, at] + other_ref[:, at].astype(F32)).astype(BF16)
        d_probs = dot(d_ctx, v, NT)
        dv_ref[:, at] = dot(probs.astype(BF16), d_ctx, TN).astype(BF16)
        inner = jnp.sum(probs * d_probs, axis=-1, keepdims=True)
        d_scores = (probs * (d_probs - inner)).astype(BF16)
        dq_ref[:, at] = (dot(d_scores, k, NN) * scale).astype(BF16)
        dk_ref[:, at] = (dot(d_scores, q, TN) * scale).astype(BF16)


def plane_slot(plane, group):
    return plane ^ (lax.axis_index("blk") // group)


def unit_kernel(own_ref, other_ref, unit_ref):
    half, count = unit_ref.shape[0], own_ref.shape[0]
    core = lax.rem(lax.axis_index("blk"), 2)
    own, other = own_ref[...].T, other_ref[...].T
    for side in range(2):

        @pl.when(core == side)
        def _():
            rows = slice(side * half, (side + 1) * half)
            unit_ref[:, :count] = own[rows]
            unit_ref[:, count:] = other[rows]


def make_unit(own, other, strips):
    count, width = own.shape
    half = width // 2
    if strips == 1:
        return call(unit_kernel, (shape(half, 2 * count),), own, other)[0]
    core = lax.rem(lax.axis_index("blk"), 2)
    both = jnp.concatenate([own, other], axis=0).T.reshape(strips, 2, half // strips, 2 * count)
    return lax.dynamic_index_in_dim(both, core, 1, keepdims=False).reshape(half, 2 * count)


def is_inner(z):
    return (z == 1) | (z == 2)


def own_bits():
    core = lax.rem(lax.axis_index("blk"), 2)
    return 1 + core, 2 - core


def late_slot(group):
    return plane_slot(lax.axis_index("shard") ^ 3, group)


def project_part(w_ref, ctx_ref, plane, group):
    return dot(w_ref[plane_slot(plane, group)], ctx_ref[...], NT)


def choose(condition, then, other):
    pl.when(condition)(then)
    pl.when(~condition)(other)


def first_message_kernel(group, own_w, near_w, soon_w, own_ref, other_ref, passing_ref, out_ref):
    count = own_ref.shape[0]
    z, slot, first = lax.axis_index("shard"), late_slot(group), own_bits()[0]

    def share(w_ref):
        for i, ctx_ref in enumerate((own_ref, other_ref)):
            out_ref[:, pl.ds(i * count, count)] = dot(w_ref[...], ctx_ref[...], NT).astype(BF16)

    @pl.when(is_inner(z))
    def _():
        out_ref[...] = passing_ref[...]

    for place, w_ref in (
        (slot == 0, own_w),
        (slot == first, near_w),
        ((slot != 0) & (slot != first), soon_w),
    ):
        pl.when(~is_inner(z) & place)(lambda w_ref=w_ref: share(w_ref))


def all_columns_kernel(group, own_w, near_w, soon_w, last_w, out_ref):
    first, second = own_bits()
    out_ref[0] = own_w[...]
    out_ref[first] = near_w[...]
    far_soon = (late_slot(group) & first) == first
    out_ref[jnp.where(far_soon, 3, second)] = soon_w[...]
    out_ref[jnp.where(far_soon, second, 3)] = last_w[...]


def second_message_kernel(group, w_ref, own_ref, other_ref, passing_ref, out_ref):
    count = own_ref.shape[0]
    z = lax.axis_index("shard")

    @pl.when(is_inner(z))
    def _():
        out_ref[...] = passing_ref[...]

    @pl.when(~is_inner(z))
    def _():
        for i, ctx_ref in enumerate((own_ref, other_ref)):
            part = project_part(w_ref, ctx_ref, z ^ 2, group)
            out_ref[:, pl.ds(i * count, count)] = part.astype(BF16)


def message_kernel(flip, group, w_ref, own_ref, other_ref, past_ref, out_ref):
    count = own_ref.shape[0]
    z = lax.axis_index("shard")
    for i, ctx_ref in enumerate((own_ref, other_ref)):
        at = pl.ds(i * count, count)
        part = project_part(w_ref, ctx_ref, z ^ flip, group)
        past = jnp.where(is_inner(z), past_ref[:, at].astype(F32), 0.0)
        out_ref[:, at] = (part + past).astype(BF16)


def last_project_kernel(group, w_ref, own_ref, other_ref, pair_ref, mid_ref, keep_ref, send_ref):
    count = own_ref.shape[0]
    z = lax.axis_index("shard")
    for i, (ctx_ref, out_ref) in enumerate(((own_ref, keep_ref), (other_ref, send_ref))):
        at = pl.ds(i * count, count)
        part = project_part(w_ref, ctx_ref, z, group) + pair_ref[:, at].astype(F32)
        out_ref[...] = part + jnp.where(is_inner(z), mid_ref[:, at].astype(F32), 0.0)


def layer_out_kernel(residual_ref, keep_ref, other_ref, out_ref):
    half = keep_ref.shape[0]
    core = lax.rem(lax.axis_index("blk"), 2)
    keep, other = keep_ref[...], other_ref[...]
    for side, order in enumerate(((keep, other), (other, keep))):

        @pl.when(core == side)
        def _():
            total = jnp.concatenate(order, axis=0).T
            out_ref[...] = (residual_ref[...].astype(F32) + total).astype(BF16)


def make_layer_out(residual, keep, other, strips):
    count, width = residual.shape
    if strips == 1:
        return call(layer_out_kernel, (shape(count, width),), residual, keep, other)[0]
    core = lax.rem(lax.axis_index("blk"), 2)
    pair = jnp.stack([keep, other]).reshape(2, strips, -1, count)
    pair = jnp.where(core == 0, pair, pair[::-1])
    total = pair.transpose(1, 0, 2, 3).reshape(width, count)
    return (residual.astype(F32) + total.T).astype(BF16)


def early_planes(unit_ref, near_ref, outer_ref, inner_ref, body):
    z = lax.axis_index("shard")
    body(z, unit_ref)
    body(z ^ 1, near_ref)
    pl.when(is_inner(z))(lambda: body(z ^ 2, inner_ref))
    pl.when(~is_inner(z))(lambda: body(z ^ 2, outer_ref))


def late_plane(inner_ref, outer_ref, body):
    z = lax.axis_index("shard")
    pl.when(is_inner(z))(lambda: body(z ^ 3, inner_ref))
    pl.when(~is_inner(z))(lambda: body(z ^ 3, outer_ref))


def d_context_early_kernel(group, *refs):
    *unit_refs, w_ref, total_ref = refs
    total_ref[...] = jnp.zeros_like(total_ref)

    def body(plane, unit_ref):
        total_ref[...] += dot(unit_ref[...], w_ref[plane_slot(plane, group)], TN)

    early_planes(*unit_refs, body)


def d_context_late_kernel(group, *refs):
    inner_ref, outer_ref, w_ref, total_ref, mine_ref, send_ref = refs
    count = mine_ref.shape[0]

    def body(plane, unit_ref):
        part = dot(unit_ref[...], w_ref[plane_slot(plane, group)], TN)
        mine_ref[...] = total_ref[:count] + part[:count]
        send_ref[...] = (total_ref[count:] + part[count:]).astype(BF16)

    late_plane(inner_ref, outer_ref, body)


def weight_part(unit_ref, own_ref, other_ref):
    count = own_ref.shape[0]
    part = dot(unit_ref[:, :count], own_ref[...], NN)
    return part + dot(unit_ref[:, count:], other_ref[...], NN)


def weight_early_kernel(group, *refs):
    *unit_refs, own_ref, other_ref, send_a, send_b, keep, rest = refs
    rows = send_a.shape[0]
    late, first = late_slot(group), own_bits()[0]

    def body(plane, unit_ref):
        slot = plane_slot(plane, group)
        part = weight_part(unit_ref, own_ref, other_ref)

        def into_rest():
            rest[...] = part

        def into_send():
            send_a[...] = part[:rows].astype(BF16)
            send_b[...] = part[rows:].astype(BF16)

        def into_keep():
            keep[...] = part

        def early():
            choose((slot & first) == first, into_send, into_keep)

        choose(slot == (late ^ first), into_rest, early)

    early_planes(*unit_refs, body)


def weight_late_kernel(group, inner_ref, outer_ref, own_ref, other_ref, rest, send, keep):
    late, first = late_slot(group), own_bits()[0]
    sends = (late & first) == first

    def body(plane, unit_ref):
        part = weight_part(unit_ref, own_ref, other_ref)
        send[...] = jnp.where(sends, part, rest[...]).astype(BF16)
        keep[...] = jnp.where(sends, rest[...], part)

    late_plane(inner_ref, outer_ref, body)


def half_sum_kernel(group, early_keep, early_from_a, early_from_b, late_keep, late_from, send, left):
    rows = early_from_a.shape[0]
    second = own_bits()[1]
    goes = (late_slot(group) & second) == second
    for at, early_from in ((pl.ds(0, rows), early_from_a), (pl.ds(rows, rows), early_from_b)):
        early_sum = early_keep[at] + early_from[...].astype(F32)
        late_sum = late_keep[at] + late_from[at].astype(F32)
        send[at] = jnp.where(goes, late_sum, early_sum).astype(BF16)
        left[at] = jnp.where(goes, early_sum, late_sum)


def grad_sum_kernel(scale, left_ref, from_ref, out_ref):
    out_ref[...] = (left_ref[...] + from_ref[...].astype(F32)) * scale


def solution(mesh):
    blk, planes = mesh.shape["blk"], mesh.shape["shard"]
    assert planes == 4
    chips = blk // 2
    strips = chips // planes
    group = 2 * strips

    def swap(value, bit):
        return lax.ppermute(value, "blk", [(i, i ^ bit) for i in range(blk)])

    def core_swap(value, first):
        bits = (1, 2) if first else (2, 1)
        return lax.ppermute(value, "blk", [(i, i ^ (group * bits[i % 2])) for i in range(blk)])

    def pair_swap(value):
        return lax.ppermute(value, "shard", [(0, 1), (1, 0), (2, 3), (3, 2)])

    def mid_swap(value):
        pairs = []
        for b in range(blk):
            pairs += [(b * planes + z, b * planes + (3 - z)) for z in (1, 2)]
            pairs += [(b * planes + z, (b ^ 1) * planes + z) for z in (0, 3)]
        return lax.ppermute(value, ("blk", "shard"), pairs)

    def together(*values):
        return lax.optimization_barrier(values)

    def bound(kernel, *static):
        return lambda *refs: kernel(*static, *refs)

    def per_device(queries, key_rows, values, segment_ids, residual, out_weight, cotangent):
        count, width = queries.shape
        half = width // 2
        position = lax.axis_index("blk") // 2
        unit_flops = 4 * half * count * width
        message = shape(half, 2 * count)

        cot_other = swap(cotangent, 1)

        w_own = out_weight.T
        bit = 1
        while bit < strips:
            there = swap(w_own, 2 * bit)
            upper = (position // bit) % 2
            w_own = jnp.concatenate(
                [jnp.where(upper, there, w_own), jnp.where(upper, w_own, there)], axis=0
            )
            bit *= 2

        w_near = core_swap(w_own, True)
        unit = make_unit(cotangent, cot_other, strips)
        near, inner_far = pair_swap(unit), mid_swap(unit)

        first = own_bits()[0]
        far_soon = (late_slot(group) & first) == first
        w_soon = core_swap(jnp.where(far_soon, w_near, w_own), False)
        w_last = core_swap(jnp.where(far_soon, w_own, w_near), False)
        asked, w_near = together(queries, w_near)
        part = shape(count // 2, width)
        ctx, low, high, probs = call(
            forward_kernel,
            (shape(count, width), part, part, shape(width // HEAD, count, count, dtype=F32)),
            asked,
            key_rows,
            values,
            segment_ids,
            flops=4 * count * count * width,
        )
        near, inner_far, ctx = together(near, inner_far, ctx)
        ctx_other = jnp.concatenate([swap(low, 1), swap(high, 1)], axis=0)

        inner_next = mid_swap(near)
        out = call(
            bound(first_message_kernel, group),
            (message,),
            w_own,
            w_near,
            w_soon,
            ctx,
            ctx_other,
            inner_far,
            flops=unit_flops,
        )[0]
        pair_two = pair_swap(out)
        w_all = call(
            bound(all_columns_kernel, group),
            (shape(planes, half, width),),
            w_own,
            w_near,
            w_soon,
            w_last,
        )[0]
        sources = (w_all, ctx, ctx_other)

        out = call(
            bound(second_message_kernel, group), (message,), *sources, inner_next, flops=unit_flops
        )[0]
        pair_three = pair_swap(out)
        out, pair_two = together(out, pair_two)
        out = call(
            bound(message_kernel, 2, group), (message,), *sources, pair_two, flops=unit_flops
        )[0]
        mid_three = mid_swap(out)
        block, rest = shape(half, width), shape(half, width, dtype=F32)
        ready = (unit, near, pair_two, inner_next)
        piece = shape(half // 2, width)
        early_send_a, early_send_b, early_keep, early_rest = call(
            bound(weight_early_kernel, group),
            (piece, piece, rest, rest),
            *ready,
            ctx,
            ctx_other,
            flops=3 * unit_flops,
        )
        early_from_a, early_from_b = core_swap(early_send_a, True), core_swap(early_send_b, True)
        d_ctx_early = call(
            bound(d_context_early_kernel, group),
            (shape(2 * count, width, dtype=F32),),
            *ready,
            w_all,
            flops=3 * unit_flops,
        )[0]
        pair_three, d_ctx_early, early_rest = together(pair_three, d_ctx_early, early_rest)

        late_send, late_keep = call(
            bound(weight_late_kernel, group),
            (block, rest),
            inner_far,
            pair_three,
            ctx,
            ctx_other,
            early_rest,
            flops=unit_flops,
        )
        late_from = core_swap(late_send, True)
        mid_three, late_send = together(mid_three, late_send)
        out = call(
            bound(message_kernel, 1, group), (message,), *sources, mid_three, flops=unit_flops
        )[0]
        pair_four = pair_swap(out)
        pair_three, early_from_a, early_from_b, out = together(pair_three, early_from_a, early_from_b, out)
        out = call(
            bound(message_kernel, 3, group), (message,), *sources, pair_three, flops=unit_flops
        )[0]
        mid_four = mid_swap(out)
        d_ctx_early, out = together(d_ctx_early, out)
        mine, send = call(
            bound(d_context_late_kernel, group),
            (shape(count, width, dtype=F32), shape(count, width)),
            inner_far,
            pair_three,
            w_all,
            d_ctx_early,
            flops=unit_flops,
        )
        d_ctx_other = swap(send, 1)
        late_from, out = together(late_from, out)
        send, left = call(
            bound(half_sum_kernel, group), (block, rest), early_keep, early_from_a, early_from_b, late_keep, late_from
        )
        second_from = core_swap(send, False)

        pair_four, mid_four = together(pair_four, mid_four)
        keep, send = call(
            bound(last_project_kernel, group),
            (shape(half, count, dtype=F32),) * 2,
            *sources,
            pair_four,
            mid_four,
            flops=unit_flops,
        )
        last_other = swap(send, 1)
        mine, keep = together(mine, keep)
        d_queries, d_keys, d_values = call(
            backward_kernel,
            (shape(count, width),) * 3,
            queries,
            key_rows,
            values,
            probs,
            mine,
            d_ctx_other,
            flops=10 * count * count * width,
        )
        layer_out = make_layer_out(residual, keep, last_other, strips)
        left, layer_out = together(left, layer_out)
        total = call(
            bound(grad_sum_kernel, 1.0 / math.sqrt(count * blk)),
            (shape(half, width, dtype=F32),),
            left,
            second_from,
        )[0]
        bit = strips // 2
        while bit >= 1:
            lower, upper = jnp.split(total, 2, axis=0)
            right = (position // bit) % 2
            sent = jnp.where(right, lower, upper)
            total = jnp.where(right, upper, lower) + swap(sent, 2 * bit)
            bit //= 2

        return layer_out, total, d_queries, d_keys, d_values

    spread = P("blk", "shard")
    return jax.shard_map(
        per_device,
        mesh=mesh,
        in_specs=(spread, spread, spread, P("blk", None), spread, P("shard", "blk"), spread),
        out_specs=(spread,) * 5,
        check_vma=False,
    )
```

```python
import math

import jax
import jax.numpy as jnp
from jax import lax
from jax.experimental import pallas as pl
from jax.experimental.pallas import tpu as pltpu
from jax.sharding import PartitionSpec as P

HEAD = 128
MASKED = -1e30
F32 = jnp.float32
BF16 = jnp.bfloat16
NT = (((1,), (1,)), ((), ()))
NN = (((1,), (0,)), ((), ()))
TN = (((0,), (0,)), ((), ()))


def dot(a, b, dims):
    return lax.dot_general(a, b, dims, preferred_element_type=F32)


def call(kernel, outs, *args, flops=0):
    size = sum(math.prod(o.shape) * o.dtype.itemsize for o in (*outs, *args))
    return pl.pallas_call(
        kernel,
        out_shape=tuple(outs),
        in_specs=[pl.BlockSpec(memory_space=pltpu.VMEM)] * len(args),
        out_specs=tuple([pl.BlockSpec(memory_space=pltpu.VMEM)] * len(outs)),
        compiler_params=pltpu.CompilerParams(vmem_limit_bytes=40 * 1024 * 1024),
        cost_estimate=pl.CostEstimate(flops=flops, bytes_accessed=size, transcendentals=0),
    )(*args)


def shape(*dims, dtype=BF16):
    return jax.ShapeDtypeStruct(dims, dtype)


def visible_mask(seg_ref):
    count = seg_ref.shape[1]
    seg = jnp.broadcast_to(seg_ref[...].astype(F32), (count, count))
    rows = lax.broadcasted_iota(jnp.int32, (count, count), 0)
    cols = lax.broadcasted_iota(jnp.int32, (count, count), 1)
    return (cols <= rows) & (seg == seg.T)


def head_probs(q, k, allowed):
    scores = dot(q, k, NT) * (1.0 / math.sqrt(HEAD))
    scores = jnp.where(allowed, scores, MASKED)
    weights = jnp.exp(scores - jnp.max(scores, axis=-1, keepdims=True))
    return weights / jnp.sum(weights, axis=-1, keepdims=True)


def forward_kernel(q_ref, k_ref, v_ref, seg_ref, ctx_ref, low_ref, high_ref, probs_ref):
    allowed = visible_mask(seg_ref)
    for h in range(q_ref.shape[1] // HEAD):
        at = pl.ds(h * HEAD, HEAD)
        probs = head_probs(q_ref[:, at], k_ref[:, at], allowed)
        probs_ref[h] = probs
        ctx = dot(probs.astype(BF16), v_ref[:, at], NN).astype(BF16)
        ctx_ref[:, at] = ctx
        low_ref[:, at], high_ref[:, at] = jnp.split(ctx, 2, axis=0)


def backward_kernel(q_ref, k_ref, v_ref, probs_ref, mine_ref, other_ref, dq_ref, dk_ref, dv_ref):
    scale = 1.0 / math.sqrt(HEAD)
    for h in range(q_ref.shape[1] // HEAD):
        at = pl.ds(h * HEAD, HEAD)
        q, k, v = q_ref[:, at], k_ref[:, at], v_ref[:, at]
        probs = probs_ref[h]
        d_ctx = (mine_ref[:, at] + other_ref[:, at].astype(F32)).astype(BF16)
        d_probs = dot(d_ctx, v, NT)
        dv_ref[:, at] = dot(probs.astype(BF16), d_ctx, TN).astype(BF16)
        inner = jnp.sum(probs * d_probs, axis=-1, keepdims=True)
        d_scores = (probs * (d_probs - inner)).astype(BF16)
        dq_ref[:, at] = (dot(d_scores, k, NN) * scale).astype(BF16)
        dk_ref[:, at] = (dot(d_scores, q, TN) * scale).astype(BF16)


def plane_slot(plane, group):
    return plane ^ (lax.axis_index("blk") // group)


def own_half_kernel(own_ref, out_ref):
    half = out_ref.shape[0]
    own = own_ref[...].T
    for side in range(2):

        @pl.when(lax.rem(lax.axis_index("blk"), 2) == side)
        def _():
            out_ref[...] = own[side * half : (side + 1) * half]


def unit_kernel(own_ref, other_ref, unit_ref):
    half, count = own_ref.shape
    other = other_ref[...].T
    unit_ref[:, :count] = own_ref[...]
    for side in range(2):

        @pl.when(lax.rem(lax.axis_index("blk"), 2) == side)
        def _():
            unit_ref[:, count:] = other[side * half : (side + 1) * half]


def make_unit(own, other, strips):
    count, width = own.shape
    half = width // 2
    if strips == 1:
        kept = call(own_half_kernel, (shape(half, count),), own)[0]
        kept, other = lax.optimization_barrier((kept, other))
        return call(unit_kernel, (shape(half, 2 * count),), kept, other)[0]
    core = lax.rem(lax.axis_index("blk"), 2)
    both = jnp.concatenate([own, other], axis=0).T.reshape(strips, 2, half // strips, 2 * count)
    return lax.dynamic_index_in_dim(both, core, 1, keepdims=False).reshape(half, 2 * count)


def is_inner(z):
    return (z == 1) | (z == 2)


def own_bits():
    core = lax.rem(lax.axis_index("blk"), 2)
    return 1 + core, 2 - core


def late_slot(group):
    return plane_slot(lax.axis_index("shard") ^ 3, group)


def project_part(w_ref, ctx_ref, plane, group):
    return dot(w_ref[plane_slot(plane, group)], ctx_ref[...], NT)


def choose(condition, then, other):
    pl.when(condition)(then)
    pl.when(~condition)(other)


def first_message_kernel(group, own_w, near_w, soon_w, own_ref, other_ref, passing_ref, out_ref):
    count = own_ref.shape[0]
    z, slot, first = lax.axis_index("shard"), late_slot(group), own_bits()[0]

    def share(w_ref):
        for i, ctx_ref in enumerate((own_ref, other_ref)):
            out_ref[:, pl.ds(i * count, count)] = dot(w_ref[...], ctx_ref[...], NT).astype(BF16)

    @pl.when(is_inner(z))
    def _():
        out_ref[...] = passing_ref[...]

    for place, w_ref in (
        (slot == 0, own_w),
        (slot == first, near_w),
        ((slot != 0) & (slot != first), soon_w),
    ):
        pl.when(~is_inner(z) & place)(lambda w_ref=w_ref: share(w_ref))


def all_columns_kernel(group, own_w, near_w, soon_w, last_w, out_ref):
    first, second = own_bits()
    out_ref[0] = own_w[...]
    out_ref[first] = near_w[...]
    far_soon = (late_slot(group) & first) == first
    out_ref[jnp.where(far_soon, 3, second)] = soon_w[...]
    out_ref[jnp.where(far_soon, second, 3)] = last_w[...]


def second_message_kernel(group, w_ref, own_ref, other_ref, passing_ref, out_ref):
    count = own_ref.shape[0]
    z = lax.axis_index("shard")

    @pl.when(is_inner(z))
    def _():
        out_ref[...] = passing_ref[...]

    @pl.when(~is_inner(z))
    def _():
        for i, ctx_ref in enumerate((own_ref, other_ref)):
            part = project_part(w_ref, ctx_ref, z ^ 2, group)
            out_ref[:, pl.ds(i * count, count)] = part.astype(BF16)


def message_kernel(flip, group, w_ref, own_ref, other_ref, past_ref, out_ref):
    count = own_ref.shape[0]
    z = lax.axis_index("shard")
    for i, ctx_ref in enumerate((own_ref, other_ref)):
        at = pl.ds(i * count, count)
        part = project_part(w_ref, ctx_ref, z ^ flip, group)
        past = jnp.where(is_inner(z), past_ref[:, at].astype(F32), 0.0)
        out_ref[:, at] = (part + past).astype(BF16)


def last_project_kernel(group, w_ref, own_ref, other_ref, pair_ref, mid_ref, keep_ref, send_ref):
    count = own_ref.shape[0]
    z = lax.axis_index("shard")
    for i, (ctx_ref, out_ref) in enumerate(((own_ref, keep_ref), (other_ref, send_ref))):
        at = pl.ds(i * count, count)
        part = project_part(w_ref, ctx_ref, z, group) + pair_ref[:, at].astype(F32)
        out_ref[...] = part + jnp.where(is_inner(z), mid_ref[:, at].astype(F32), 0.0)


def layer_out_kernel(residual_ref, keep_ref, other_ref, out_ref):
    half = keep_ref.shape[0]
    core = lax.rem(lax.axis_index("blk"), 2)
    keep, other = keep_ref[...], other_ref[...]
    for side, order in enumerate(((keep, other), (other, keep))):

        @pl.when(core == side)
        def _():
            total = jnp.concatenate(order, axis=0).T
            out_ref[...] = (residual_ref[...].astype(F32) + total).astype(BF16)


def make_layer_out(residual, keep, other, strips):
    count, width = residual.shape
    if strips == 1:
        return call(layer_out_kernel, (shape(count, width),), residual, keep, other)[0]
    core = lax.rem(lax.axis_index("blk"), 2)
    pair = jnp.stack([keep, other]).reshape(2, strips, -1, count)
    pair = jnp.where(core == 0, pair, pair[::-1])
    total = pair.transpose(1, 0, 2, 3).reshape(width, count)
    return (residual.astype(F32) + total.T).astype(BF16)


def late_plane(inner_ref, outer_ref, body):
    z = lax.axis_index("shard")
    pl.when(is_inner(z))(lambda: body(z ^ 3, inner_ref))
    pl.when(~is_inner(z))(lambda: body(z ^ 3, outer_ref))


def d_context_early_kernel(group, unit_ref, near_ref, w_ref, total_ref):
    z = lax.axis_index("shard")
    total_ref[...] = dot(unit_ref[...], w_ref[plane_slot(z, group)], TN)
    total_ref[...] += dot(near_ref[...], w_ref[plane_slot(z ^ 1, group)], TN)


def d_context_late_kernel(group, *refs):
    outer_next, inner_next, inner_far, outer_far, w_ref, total_ref, mine_ref, send_ref = refs
    count = mine_ref.shape[0]
    z = lax.axis_index("shard")

    def finish(next_ref, far_ref):
        part = dot(next_ref[...], w_ref[plane_slot(z ^ 2, group)], TN)
        part = part + dot(far_ref[...], w_ref[plane_slot(z ^ 3, group)], TN)
        mine_ref[...] = total_ref[:count] + part[:count]
        send_ref[...] = (total_ref[count:] + part[count:]).astype(BF16)

    choose(is_inner(z), lambda: finish(inner_next, inner_far), lambda: finish(outer_next, outer_far))


def weight_part(unit_ref, own_ref, other_ref):
    count = own_ref.shape[0]
    part = dot(unit_ref[:, :count], own_ref[...], NN)
    return part + dot(unit_ref[:, count:], other_ref[...], NN)


def first_pair(group):
    core, first = lax.rem(lax.axis_index("blk"), 2), own_bits()[0]
    slot = plane_slot(lax.axis_index("shard"), group)
    return (slot & first) == first, core == 0


def weight_first_kernel(unit_ref, near_ref, own_ref, other_ref, here_ref, near_out):
    here_ref[...] = weight_part(unit_ref, own_ref, other_ref)
    near_out[...] = weight_part(near_ref, own_ref, other_ref)


def weight_early_kernel(group, *refs):
    outer_ref, inner_ref, own_ref, other_ref, here, near, send_a, send_b, beyond = refs
    rows = send_a.shape[0]

    def body(unit_ref):
        beyond[...] = weight_part(unit_ref, own_ref, other_ref)

    def send(block):
        send_a[...] = block[:rows].astype(BF16)
        send_b[...] = block[rows:].astype(BF16)

    choose(is_inner(lax.axis_index("shard")), lambda: body(inner_ref), lambda: body(outer_ref))
    here_goes, with_near = first_pair(group)
    pl.when(here_goes)(lambda: send(here))
    pl.when(~here_goes & with_near)(lambda: send(near))
    pl.when(~here_goes & ~with_near)(lambda: send(beyond))


def weight_late_kernel(group, inner_ref, outer_ref, own_ref, other_ref, near, beyond, send, keep):
    late, first = late_slot(group), own_bits()[0]
    sends = (late & first) == first
    rest = jnp.where(first_pair(group)[1], beyond[...], near[...])

    def body(plane, unit_ref):
        part = weight_part(unit_ref, own_ref, other_ref)
        send[...] = jnp.where(sends, part, rest).astype(BF16)
        keep[...] = jnp.where(sends, rest, part)

    late_plane(inner_ref, outer_ref, body)


def half_sum_kernel(group, here, near, beyond, from_a, from_b, late_keep, late_from, send, left):
    rows = from_a.shape[0]
    second = own_bits()[1]
    goes = (late_slot(group) & second) == second
    here_goes, with_near = first_pair(group)

    def add(early_keep):
        for at, early_from in ((pl.ds(0, rows), from_a), (pl.ds(rows, rows), from_b)):
            early_sum = early_keep[at] + early_from[...].astype(F32)
            late_sum = late_keep[at] + late_from[at].astype(F32)
            send[at] = jnp.where(goes, late_sum, early_sum).astype(BF16)
            left[at] = jnp.where(goes, early_sum, late_sum)

    pl.when(~here_goes)(lambda: add(here))
    pl.when(here_goes & with_near)(lambda: add(near))
    pl.when(here_goes & ~with_near)(lambda: add(beyond))


def grad_sum_kernel(scale, left_ref, from_ref, out_ref):
    out_ref[...] = (left_ref[...] + from_ref[...].astype(F32)) * scale


def solution(mesh):
    blk, planes = mesh.shape["blk"], mesh.shape["shard"]
    assert planes == 4
    chips = blk // 2
    strips = chips // planes
    group = 2 * strips

    def swap(value, bit):
        return lax.ppermute(value, "blk", [(i, i ^ bit) for i in range(blk)])

    def core_swap(value, first):
        bits = (1, 2) if first else (2, 1)
        return lax.ppermute(value, "blk", [(i, i ^ (group * bits[i % 2])) for i in range(blk)])

    def pair_swap(value):
        return lax.ppermute(value, "shard", [(0, 1), (1, 0), (2, 3), (3, 2)])

    def mid_swap(value):
        pairs = []
        for b in range(blk):
            pairs += [(b * planes + z, b * planes + (3 - z)) for z in (1, 2)]
            pairs += [(b * planes + z, (b ^ 1) * planes + z) for z in (0, 3)]
        return lax.ppermute(value, ("blk", "shard"), pairs)

    def together(*values):
        return lax.optimization_barrier(values)

    def bound(kernel, *static):
        return lambda *refs: kernel(*static, *refs)

    def per_device(queries, key_rows, values, segment_ids, residual, out_weight, cotangent):
        count, width = queries.shape
        half = width // 2
        position = lax.axis_index("blk") // 2
        unit_flops = 4 * half * count * width
        message = shape(half, 2 * count)

        cot_other = swap(cotangent, 1)

        w_own = out_weight.T
        bit = 1
        while bit < strips:
            there = swap(w_own, 2 * bit)
            upper = (position // bit) % 2
            w_own = jnp.concatenate(
                [jnp.where(upper, there, w_own), jnp.where(upper, w_own, there)], axis=0
            )
            bit *= 2

        w_near = core_swap(w_own, True)
        unit = make_unit(cotangent, cot_other, strips)
        near, inner_far = pair_swap(unit), mid_swap(unit)

        first = own_bits()[0]
        far_soon = (late_slot(group) & first) == first
        w_soon = core_swap(jnp.where(far_soon, w_near, w_own), False)
        w_last = core_swap(jnp.where(far_soon, w_own, w_near), False)
        asked, w_near = together(queries, w_near)
        part = shape(count // 2, width)
        ctx, low, high, probs = call(
            forward_kernel,
            (shape(count, width), part, part, shape(width // HEAD, count, count, dtype=F32)),
            asked,
            key_rows,
            values,
            segment_ids,
            flops=4 * count * count * width,
        )
        near, inner_far, ctx = together(near, inner_far, ctx)
        ctx_other = jnp.concatenate([swap(low, 1), swap(high, 1)], axis=0)

        inner_next = mid_swap(near)
        out = call(
            bound(first_message_kernel, group),
            (message,),
            w_own,
            w_near,
            w_soon,
            ctx,
            ctx_other,
            inner_far,
            flops=unit_flops,
        )[0]
        pair_two = pair_swap(out)
        w_all = call(
            bound(all_columns_kernel, group),
            (shape(planes, half, width),),
            w_own,
            w_near,
            w_soon,
            w_last,
        )[0]
        sources = (w_all, ctx, ctx_other)
        d_ctx_early = call(
            bound(d_context_early_kernel, group),
            (shape(2 * count, width, dtype=F32),),
            unit,
            near,
            w_all,
            flops=2 * unit_flops,
        )[0]
        block, rest = shape(half, width), shape(half, width, dtype=F32)
        here_part, near_part = call(
            weight_first_kernel, (rest, rest), unit, near, ctx, ctx_other, flops=2 * unit_flops
        )
        inner_next, d_ctx_early, here_part = together(inner_next, d_ctx_early, here_part)

        out = call(
            bound(second_message_kernel, group), (message,), *sources, inner_next, flops=unit_flops
        )[0]
        pair_three = pair_swap(out)
        out, pair_two = together(out, pair_two)
        out = call(
            bound(message_kernel, 2, group), (message,), *sources, pair_two, flops=unit_flops
        )[0]
        mid_three = mid_swap(out)
        piece = shape(half // 2, width)
        early_send_a, early_send_b, beyond_part = call(
            bound(weight_early_kernel, group),
            (piece, piece, rest),
            pair_two,
            inner_next,
            ctx,
            ctx_other,
            here_part,
            near_part,
            flops=unit_flops,
        )
        early_from_a, early_from_b = core_swap(early_send_a, True), core_swap(early_send_b, True)
        pair_three, beyond_part = together(pair_three, beyond_part)

        late_send, late_keep = call(
            bound(weight_late_kernel, group),
            (block, rest),
            inner_far,
            pair_three,
            ctx,
            ctx_other,
            near_part,
            beyond_part,
            flops=unit_flops,
        )
        late_from = core_swap(late_send, True)
        mid_three, late_send = together(mid_three, late_send)
        out = call(
            bound(message_kernel, 1, group), (message,), *sources, mid_three, flops=unit_flops
        )[0]
        pair_four = pair_swap(out)
        pair_three, early_from_a, early_from_b, out = together(pair_three, early_from_a, early_from_b, out)
        out = call(
            bound(message_kernel, 3, group), (message,), *sources, pair_three, flops=unit_flops
        )[0]
        mid_four = mid_swap(out)
        d_ctx_early, out = together(d_ctx_early, out)
        mine, send = call(
            bound(d_context_late_kernel, group),
            (shape(count, width, dtype=F32), shape(count, width)),
            pair_two,
            inner_next,
            inner_far,
            pair_three,
            w_all,
            d_ctx_early,
            flops=2 * unit_flops,
        )
        d_ctx_other = swap(send, 1)
        late_from, out = together(late_from, out)
        send, left = call(
            bound(half_sum_kernel, group),
            (block, rest),
            here_part,
            near_part,
            beyond_part,
            early_from_a,
            early_from_b,
            late_keep,
            late_from,
        )
        second_from = core_swap(send, False)

        pair_four, mid_four = together(pair_four, mid_four)
        keep, send = call(
            bound(last_project_kernel, group),
            (shape(half, count, dtype=F32),) * 2,
            *sources,
            pair_four,
            mid_four,
            flops=unit_flops,
        )
        last_other = swap(send, 1)
        mine, keep = together(mine, keep)
        d_queries, d_keys, d_values = call(
            backward_kernel,
            (shape(count, width),) * 3,
            queries,
            key_rows,
            values,
            probs,
            mine,
            d_ctx_other,
            flops=10 * count * count * width,
        )
        layer_out = make_layer_out(residual, keep, last_other, strips)
        left, layer_out = together(left, layer_out)
        total = call(
            bound(grad_sum_kernel, 1.0 / math.sqrt(count * blk)),
            (shape(half, width, dtype=F32),),
            left,
            second_from,
        )[0]
        bit = strips // 2
        while bit >= 1:
            lower, upper = jnp.split(total, 2, axis=0)
            right = (position // bit) % 2
            sent = jnp.where(right, lower, upper)
            total = jnp.where(right, upper, lower) + swap(sent, 2 * bit)
            bit //= 2

        return layer_out, total, d_queries, d_keys, d_values

    spread = P("blk", "shard")
    return jax.shard_map(
        per_device,
        mesh=mesh,
        in_specs=(spread, spread, spread, P("blk", None), spread, P("shard", "blk"), spread),
        out_specs=(spread,) * 5,
        check_vma=False,
    )
```

```python
import math

import jax
import jax.numpy as jnp
from jax import lax
from jax.experimental import pallas as pl
from jax.experimental.pallas import tpu as pltpu
from jax.sharding import PartitionSpec as P

HEAD = 128
MASKED = -1e30
F32 = jnp.float32
BF16 = jnp.bfloat16
NT = (((1,), (1,)), ((), ()))
NN = (((1,), (0,)), ((), ()))
TN = (((0,), (0,)), ((), ()))


def dot(a, b, dims):
    return lax.dot_general(a, b, dims, preferred_element_type=F32)


def call(kernel, outs, *args, flops=0):
    size = sum(math.prod(o.shape) * o.dtype.itemsize for o in (*outs, *args))
    return pl.pallas_call(
        kernel,
        out_shape=tuple(outs),
        in_specs=[pl.BlockSpec(memory_space=pltpu.VMEM)] * len(args),
        out_specs=tuple([pl.BlockSpec(memory_space=pltpu.VMEM)] * len(outs)),
        compiler_params=pltpu.CompilerParams(vmem_limit_bytes=40 * 1024 * 1024),
        cost_estimate=pl.CostEstimate(flops=flops, bytes_accessed=size, transcendentals=0),
    )(*args)


def shape(*dims, dtype=BF16):
    return jax.ShapeDtypeStruct(dims, dtype)


def visible_mask(seg_ref):
    count = seg_ref.shape[1]
    seg = jnp.broadcast_to(seg_ref[...].astype(F32), (count, count))
    rows = lax.broadcasted_iota(jnp.int32, (count, count), 0)
    cols = lax.broadcasted_iota(jnp.int32, (count, count), 1)
    return (cols <= rows) & (seg == seg.T)


def head_probs(q, k, allowed):
    scores = dot(q, k, NT) * (1.0 / math.sqrt(HEAD))
    scores = jnp.where(allowed, scores, MASKED)
    weights = jnp.exp(scores - jnp.max(scores, axis=-1, keepdims=True))
    return weights / jnp.sum(weights, axis=-1, keepdims=True)


def forward_kernel(q_ref, k_ref, v_ref, seg_ref, ctx_ref, low_ref, high_ref, probs_ref):
    allowed = visible_mask(seg_ref)
    for h in range(q_ref.shape[1] // HEAD):
        at = pl.ds(h * HEAD, HEAD)
        probs = head_probs(q_ref[:, at], k_ref[:, at], allowed)
        probs_ref[h] = probs
        ctx = dot(probs.astype(BF16), v_ref[:, at], NN).astype(BF16)
        ctx_ref[:, at] = ctx
        low_ref[:, at], high_ref[:, at] = jnp.split(ctx, 2, axis=0)


def backward_kernel(q_ref, k_ref, v_ref, probs_ref, mine_ref, other_ref, dq_ref, dk_ref, dv_ref):
    scale = 1.0 / math.sqrt(HEAD)
    for h in range(q_ref.shape[1] // HEAD):
        at = pl.ds(h * HEAD, HEAD)
        q, k, v = q_ref[:, at], k_ref[:, at], v_ref[:, at]
        probs = probs_ref[h]
        d_ctx = (mine_ref[:, at] + other_ref[:, at].astype(F32)).astype(BF16)
        d_probs = dot(d_ctx, v, NT)
        dv_ref[:, at] = dot(probs.astype(BF16), d_ctx, TN).astype(BF16)
        inner = jnp.sum(probs * d_probs, axis=-1, keepdims=True)
        d_scores = (probs * (d_probs - inner)).astype(BF16)
        dq_ref[:, at] = (dot(d_scores, k, NN) * scale).astype(BF16)
        dk_ref[:, at] = (dot(d_scores, q, TN) * scale).astype(BF16)


def plane_slot(plane, group):
    return plane ^ (lax.axis_index("blk") // group)


def own_half_kernel(own_ref, out_ref):
    half = out_ref.shape[0]
    own = own_ref[...].T
    for side in range(2):

        @pl.when(lax.rem(lax.axis_index("blk"), 2) == side)
        def _():
            out_ref[...] = own[side * half : (side + 1) * half]


def unit_kernel(own_ref, other_ref, unit_ref):
    half, count = own_ref.shape
    other = other_ref[...].T
    unit_ref[:, :count] = own_ref[...]
    for side in range(2):

        @pl.when(lax.rem(lax.axis_index("blk"), 2) == side)
        def _():
            unit_ref[:, count:] = other[side * half : (side + 1) * half]


def make_unit(own, other, strips):
    count, width = own.shape
    half = width // 2
    if strips == 1:
        kept = call(own_half_kernel, (shape(half, count),), own)[0]
        kept, other = lax.optimization_barrier((kept, other))
        return call(unit_kernel, (shape(half, 2 * count),), kept, other)[0]
    core = lax.rem(lax.axis_index("blk"), 2)
    both = jnp.concatenate([own, other], axis=0).T.reshape(strips, 2, half // strips, 2 * count)
    return lax.dynamic_index_in_dim(both, core, 1, keepdims=False).reshape(half, 2 * count)


def is_inner(z):
    return (z == 1) | (z == 2)


def own_bits():
    core = lax.rem(lax.axis_index("blk"), 2)
    return 1 + core, 2 - core


def late_slot(group):
    return plane_slot(lax.axis_index("shard") ^ 3, group)


def project_part(w_ref, ctx_ref, plane, group):
    return dot(w_ref[plane_slot(plane, group)], ctx_ref[...], NT)


def choose(condition, then, other):
    pl.when(condition)(then)
    pl.when(~condition)(other)


def first_message_kernel(group, own_w, near_w, soon_w, own_ref, other_ref, passing_ref, out_ref):
    count = own_ref.shape[0]
    z, slot, first = lax.axis_index("shard"), late_slot(group), own_bits()[0]

    def share(w_ref):
        for i, ctx_ref in enumerate((own_ref, other_ref)):
            out_ref[:, pl.ds(i * count, count)] = dot(w_ref[...], ctx_ref[...], NT).astype(BF16)

    @pl.when(is_inner(z))
    def _():
        out_ref[...] = passing_ref[...]

    for place, w_ref in (
        (slot == 0, own_w),
        (slot == first, near_w),
        ((slot != 0) & (slot != first), soon_w),
    ):
        pl.when(~is_inner(z) & place)(lambda w_ref=w_ref: share(w_ref))


def all_columns_kernel(group, own_w, near_w, soon_w, last_w, out_ref):
    first, second = own_bits()
    out_ref[0] = own_w[...]
    out_ref[first] = near_w[...]
    far_soon = (late_slot(group) & first) == first
    out_ref[jnp.where(far_soon, 3, second)] = soon_w[...]
    out_ref[jnp.where(far_soon, second, 3)] = last_w[...]


def second_message_kernel(group, w_ref, own_ref, other_ref, passing_ref, out_ref):
    count = own_ref.shape[0]
    z = lax.axis_index("shard")

    @pl.when(is_inner(z))
    def _():
        out_ref[...] = passing_ref[...]

    @pl.when(~is_inner(z))
    def _():
        for i, ctx_ref in enumerate((own_ref, other_ref)):
            part = project_part(w_ref, ctx_ref, z ^ 2, group)
            out_ref[:, pl.ds(i * count, count)] = part.astype(BF16)


def message_kernel(flip, group, w_ref, own_ref, other_ref, past_ref, out_ref):
    count = own_ref.shape[0]
    z = lax.axis_index("shard")
    for i, ctx_ref in enumerate((own_ref, other_ref)):
        at = pl.ds(i * count, count)
        part = project_part(w_ref, ctx_ref, z ^ flip, group)
        past = jnp.where(is_inner(z), past_ref[:, at].astype(F32), 0.0)
        out_ref[:, at] = (part + past).astype(BF16)


def last_project_kernel(group, w_ref, own_ref, other_ref, pair_ref, mid_ref, keep_ref, send_ref):
    count = own_ref.shape[0]
    z = lax.axis_index("shard")
    for i, (ctx_ref, out_ref) in enumerate(((own_ref, keep_ref), (other_ref, send_ref))):
        at = pl.ds(i * count, count)
        part = project_part(w_ref, ctx_ref, z, group) + pair_ref[:, at].astype(F32)
        out_ref[...] = part + jnp.where(is_inner(z), mid_ref[:, at].astype(F32), 0.0)


def layer_out_kernel(residual_ref, keep_ref, other_ref, out_ref):
    half = keep_ref.shape[0]
    core = lax.rem(lax.axis_index("blk"), 2)
    keep, other = keep_ref[...], other_ref[...]
    for side, order in enumerate(((keep, other), (other, keep))):

        @pl.when(core == side)
        def _():
            total = jnp.concatenate(order, axis=0).T
            out_ref[...] = (residual_ref[...].astype(F32) + total).astype(BF16)


def make_layer_out(residual, keep, other, strips):
    count, width = residual.shape
    if strips == 1:
        return call(layer_out_kernel, (shape(count, width),), residual, keep, other)[0]
    core = lax.rem(lax.axis_index("blk"), 2)
    pair = jnp.stack([keep, other]).reshape(2, strips, -1, count)
    pair = jnp.where(core == 0, pair, pair[::-1])
    total = pair.transpose(1, 0, 2, 3).reshape(width, count)
    return (residual.astype(F32) + total.T).astype(BF16)


def late_plane(inner_ref, outer_ref, body):
    z = lax.axis_index("shard")
    pl.when(is_inner(z))(lambda: body(z ^ 3, inner_ref))
    pl.when(~is_inner(z))(lambda: body(z ^ 3, outer_ref))


def d_context_early_kernel(group, unit_ref, near_ref, w_ref, total_ref):
    z = lax.axis_index("shard")
    total_ref[...] = dot(unit_ref[...], w_ref[plane_slot(z, group)], TN)
    total_ref[...] += dot(near_ref[...], w_ref[plane_slot(z ^ 1, group)], TN)


def d_context_late_kernel(group, *refs):
    outer_next, inner_next, inner_far, outer_far, w_ref, total_ref, mine_ref, send_ref = refs
    count = mine_ref.shape[0]
    z = lax.axis_index("shard")

    def finish(next_ref, far_ref):
        part = dot(next_ref[...], w_ref[plane_slot(z ^ 2, group)], TN)
        part = part + dot(far_ref[...], w_ref[plane_slot(z ^ 3, group)], TN)
        mine_ref[...] = total_ref[:count] + part[:count]
        send_ref[...] = (total_ref[count:] + part[count:]).astype(BF16)

    choose(is_inner(z), lambda: finish(inner_next, inner_far), lambda: finish(outer_next, outer_far))


def weight_part(unit_ref, own_ref, other_ref):
    count = own_ref.shape[0]
    part = dot(unit_ref[:, :count], own_ref[...], NN)
    return part + dot(unit_ref[:, count:], other_ref[...], NN)


def first_pair(group):
    core, first = lax.rem(lax.axis_index("blk"), 2), own_bits()[0]
    slot = plane_slot(lax.axis_index("shard"), group)
    return (slot & first) == first, core == 0


def weight_first_kernel(unit_ref, near_ref, own_ref, other_ref, here_ref, near_out):
    here_ref[...] = weight_part(unit_ref, own_ref, other_ref)
    near_out[...] = weight_part(near_ref, own_ref, other_ref)


def weight_early_kernel(group, *refs):
    outer_ref, inner_ref, own_ref, other_ref, here, near, send_a, send_b, beyond = refs
    rows = send_a.shape[0]

    def body(unit_ref):
        beyond[...] = weight_part(unit_ref, own_ref, other_ref)

    def send(block):
        send_a[...] = block[:rows].astype(BF16)
        send_b[...] = block[rows:].astype(BF16)

    choose(is_inner(lax.axis_index("shard")), lambda: body(inner_ref), lambda: body(outer_ref))
    here_goes, with_near = first_pair(group)
    pl.when(here_goes)(lambda: send(here))
    pl.when(~here_goes & with_near)(lambda: send(near))
    pl.when(~here_goes & ~with_near)(lambda: send(beyond))


def weight_late_kernel(group, inner_ref, outer_ref, own_ref, other_ref, near, beyond, send, keep):
    late, first = late_slot(group), own_bits()[0]
    sends = (late & first) == first
    rest = jnp.where(first_pair(group)[1], beyond[...], near[...])

    def body(plane, unit_ref):
        part = weight_part(unit_ref, own_ref, other_ref)
        send[...] = jnp.where(sends, part, rest).astype(BF16)
        keep[...] = jnp.where(sends, rest, part)

    late_plane(inner_ref, outer_ref, body)


def half_sum_kernel(group, here, near, beyond, from_a, from_b, late_keep, late_from, send, left):
    rows = from_a.shape[0]
    second = own_bits()[1]
    goes = (late_slot(group) & second) == second
    here_goes, with_near = first_pair(group)

    def add(early_keep):
        for at, early_from in ((pl.ds(0, rows), from_a), (pl.ds(rows, rows), from_b)):
            early_sum = early_keep[at] + early_from[...].astype(F32)
            late_sum = late_keep[at] + late_from[at].astype(F32)
            send[at] = jnp.where(goes, late_sum, early_sum).astype(BF16)
            left[at] = jnp.where(goes, early_sum, late_sum)

    pl.when(~here_goes)(lambda: add(here))
    pl.when(here_goes & with_near)(lambda: add(near))
    pl.when(here_goes & ~with_near)(lambda: add(beyond))


def grad_sum_kernel(scale, left_ref, from_ref, out_ref):
    out_ref[...] = (left_ref[...] + from_ref[...].astype(F32)) * scale


def solution(mesh):
    blk, planes = mesh.shape["blk"], mesh.shape["shard"]
    assert planes == 4
    chips = blk // 2
    strips = chips // planes
    group = 2 * strips

    def swap(value, bit):
        return lax.ppermute(value, "blk", [(i, i ^ bit) for i in range(blk)])

    def core_swap(value, first):
        bits = (1, 2) if first else (2, 1)
        return lax.ppermute(value, "blk", [(i, i ^ (group * bits[i % 2])) for i in range(blk)])

    def pair_swap(value):
        return lax.ppermute(value, "shard", [(0, 1), (1, 0), (2, 3), (3, 2)])

    def mid_swap(value):
        pairs = []
        for b in range(blk):
            pairs += [(b * planes + z, b * planes + (3 - z)) for z in (1, 2)]
            pairs += [(b * planes + z, (b ^ 1) * planes + z) for z in (0, 3)]
        return lax.ppermute(value, ("blk", "shard"), pairs)

    def together(*values):
        return lax.optimization_barrier(values)

    def bound(kernel, *static):
        return lambda *refs: kernel(*static, *refs)

    def per_device(queries, key_rows, values, segment_ids, residual, out_weight, cotangent):
        count, width = queries.shape
        half = width // 2
        position = lax.axis_index("blk") // 2
        unit_flops = 4 * half * count * width
        message = shape(half, 2 * count)

        cot_other = swap(cotangent, 1)

        w_own = out_weight.T
        bit = 1
        while bit < strips:
            there = swap(w_own, 2 * bit)
            upper = (position // bit) % 2
            w_own = jnp.concatenate(
                [jnp.where(upper, there, w_own), jnp.where(upper, w_own, there)], axis=0
            )
            bit *= 2

        w_near = core_swap(w_own, True)
        unit = make_unit(cotangent, cot_other, strips)
        inner_far, near = mid_swap(unit), pair_swap(unit)

        first = own_bits()[0]
        far_soon = (late_slot(group) & first) == first
        w_soon = core_swap(jnp.where(far_soon, w_near, w_own), False)
        w_last = core_swap(jnp.where(far_soon, w_own, w_near), False)
        asked, w_near = together(queries, w_near)
        part = shape(count // 2, width)
        ctx, low, high, probs = call(
            forward_kernel,
            (shape(count, width), part, part, shape(width // HEAD, count, count, dtype=F32)),
            asked,
            key_rows,
            values,
            segment_ids,
            flops=4 * count * count * width,
        )
        near, inner_far, ctx = together(near, inner_far, ctx)
        ctx_other = jnp.concatenate([swap(low, 1), swap(high, 1)], axis=0)

        inner_next = mid_swap(near)
        out = call(
            bound(first_message_kernel, group),
            (message,),
            w_own,
            w_near,
            w_soon,
            ctx,
            ctx_other,
            inner_far,
            flops=unit_flops,
        )[0]
        pair_two = pair_swap(out)
        w_all = call(
            bound(all_columns_kernel, group),
            (shape(planes, half, width),),
            w_own,
            w_near,
            w_soon,
            w_last,
        )[0]
        sources = (w_all, ctx, ctx_other)
        d_ctx_early = call(
            bound(d_context_early_kernel, group),
            (shape(2 * count, width, dtype=F32),),
            unit,
            near,
            w_all,
            flops=2 * unit_flops,
        )[0]
        block, rest = shape(half, width), shape(half, width, dtype=F32)
        here_part, near_part = call(
            weight_first_kernel, (rest, rest), unit, near, ctx, ctx_other, flops=2 * unit_flops
        )
        inner_next, d_ctx_early, here_part = together(inner_next, d_ctx_early, here_part)

        out = call(
            bound(second_message_kernel, group), (message,), *sources, inner_next, flops=unit_flops
        )[0]
        pair_three = pair_swap(out)
        out, pair_two = together(out, pair_two)
        out = call(
            bound(message_kernel, 2, group), (message,), *sources, pair_two, flops=unit_flops
        )[0]
        mid_three = mid_swap(out)
        piece = shape(half // 2, width)
        early_send_a, early_send_b, beyond_part = call(
            bound(weight_early_kernel, group),
            (piece, piece, rest),
            pair_two,
            inner_next,
            ctx,
            ctx_other,
            here_part,
            near_part,
            flops=unit_flops,
        )
        early_from_a, early_from_b = core_swap(early_send_a, True), core_swap(early_send_b, True)
        pair_three, beyond_part = together(pair_three, beyond_part)

        late_send, late_keep = call(
            bound(weight_late_kernel, group),
            (block, rest),
            inner_far,
            pair_three,
            ctx,
            ctx_other,
            near_part,
            beyond_part,
            flops=unit_flops,
        )
        late_from = core_swap(late_send, True)
        mid_three, late_send = together(mid_three, late_send)
        out = call(
            bound(message_kernel, 1, group), (message,), *sources, mid_three, flops=unit_flops
        )[0]
        pair_four = pair_swap(out)
        pair_three, early_from_a, early_from_b, out = together(pair_three, early_from_a, early_from_b, out)
        out = call(
            bound(message_kernel, 3, group), (message,), *sources, pair_three, flops=unit_flops
        )[0]
        mid_four = mid_swap(out)
        d_ctx_early, out = together(d_ctx_early, out)
        mine, send = call(
            bound(d_context_late_kernel, group),
            (shape(count, width, dtype=F32), shape(count, width)),
            pair_two,
            inner_next,
            inner_far,
            pair_three,
            w_all,
            d_ctx_early,
            flops=2 * unit_flops,
        )
        d_ctx_other = swap(send, 1)
        late_from, out = together(late_from, out)
        send, left = call(
            bound(half_sum_kernel, group),
            (block, rest),
            here_part,
            near_part,
            beyond_part,
            early_from_a,
            early_from_b,
            late_keep,
            late_from,
        )
        second_from = core_swap(send, False)

        pair_four, mid_four = together(pair_four, mid_four)
        keep, send = call(
            bound(last_project_kernel, group),
            (shape(half, count, dtype=F32),) * 2,
            *sources,
            pair_four,
            mid_four,
            flops=unit_flops,
        )
        last_other = swap(send, 1)
        mine, keep = together(mine, keep)
        d_queries, d_keys, d_values = call(
            backward_kernel,
            (shape(count, width),) * 3,
            queries,
            key_rows,
            values,
            probs,
            mine,
            d_ctx_other,
            flops=10 * count * count * width,
        )
        layer_out = make_layer_out(residual, keep, last_other, strips)
        left, layer_out = together(left, layer_out)
        total = call(
            bound(grad_sum_kernel, 1.0 / math.sqrt(count * blk)),
            (shape(half, width, dtype=F32),),
            left,
            second_from,
        )[0]
        bit = strips // 2
        while bit >= 1:
            lower, upper = jnp.split(total, 2, axis=0)
            right = (position // bit) % 2
            sent = jnp.where(right, lower, upper)
            total = jnp.where(right, upper, lower) + swap(sent, 2 * bit)
            bit //= 2

        return layer_out, total, d_queries, d_keys, d_values

    spread = P("blk", "shard")
    return jax.shard_map(
        per_device,
        mesh=mesh,
        in_specs=(spread, spread, spread, P("blk", None), spread, P("shard", "blk"), spread),
        out_specs=(spread,) * 5,
        check_vma=False,
    )
```

```python
import math

import jax
import jax.numpy as jnp
from jax import lax
from jax.experimental import pallas as pl
from jax.experimental.pallas import tpu as pltpu
from jax.sharding import PartitionSpec as P

HEAD = 128
MASKED = -1e30
F32 = jnp.float32
BF16 = jnp.bfloat16
NT = (((1,), (1,)), ((), ()))
NN = (((1,), (0,)), ((), ()))
TN = (((0,), (0,)), ((), ()))


def dot(a, b, dims):
    return lax.dot_general(a, b, dims, preferred_element_type=F32)


def call(kernel, outs, *args, flops=0):
    size = sum(math.prod(o.shape) * o.dtype.itemsize for o in (*outs, *args))
    return pl.pallas_call(
        kernel,
        out_shape=tuple(outs),
        in_specs=[pl.BlockSpec(memory_space=pltpu.VMEM)] * len(args),
        out_specs=tuple([pl.BlockSpec(memory_space=pltpu.VMEM)] * len(outs)),
        compiler_params=pltpu.CompilerParams(vmem_limit_bytes=40 * 1024 * 1024),
        cost_estimate=pl.CostEstimate(flops=flops, bytes_accessed=size, transcendentals=0),
    )(*args)


def shape(*dims, dtype=BF16):
    return jax.ShapeDtypeStruct(dims, dtype)


def visible_mask(seg_ref):
    count = seg_ref.shape[1]
    seg = jnp.broadcast_to(seg_ref[...].astype(F32), (count, count))
    rows = lax.broadcasted_iota(jnp.int32, (count, count), 0)
    cols = lax.broadcasted_iota(jnp.int32, (count, count), 1)
    return (cols <= rows) & (seg == seg.T)


def head_probs(q, k, allowed):
    scores = dot(q, k, NT) * (1.0 / math.sqrt(HEAD))
    scores = jnp.where(allowed, scores, MASKED)
    weights = jnp.exp(scores - jnp.max(scores, axis=-1, keepdims=True))
    return weights / jnp.sum(weights, axis=-1, keepdims=True)


def forward_kernel(q_ref, k_ref, v_ref, seg_ref, ctx_ref, low_ref, high_ref, probs_ref):
    allowed = visible_mask(seg_ref)
    for h in range(q_ref.shape[1] // HEAD):
        at = pl.ds(h * HEAD, HEAD)
        probs = head_probs(q_ref[:, at], k_ref[:, at], allowed)
        probs_ref[h] = probs
        ctx = dot(probs.astype(BF16), v_ref[:, at], NN).astype(BF16)
        ctx_ref[:, at] = ctx
        low_ref[:, at], high_ref[:, at] = jnp.split(ctx, 2, axis=0)


def backward_kernel(q_ref, k_ref, v_ref, probs_ref, mine_ref, other_ref, dq_ref, dk_ref, dv_ref):
    scale = 1.0 / math.sqrt(HEAD)
    for h in range(q_ref.shape[1] // HEAD):
        at = pl.ds(h * HEAD, HEAD)
        q, k, v = q_ref[:, at], k_ref[:, at], v_ref[:, at]
        probs = probs_ref[h]
        d_ctx = (mine_ref[:, at] + other_ref[:, at].astype(F32)).astype(BF16)
        d_probs = dot(d_ctx, v, NT)
        dv_ref[:, at] = dot(probs.astype(BF16), d_ctx, TN).astype(BF16)
        inner = jnp.sum(probs * d_probs, axis=-1, keepdims=True)
        d_scores = (probs * (d_probs - inner)).astype(BF16)
        dq_ref[:, at] = (dot(d_scores, k, NN) * scale).astype(BF16)
        dk_ref[:, at] = (dot(d_scores, q, TN) * scale).astype(BF16)


def plane_slot(plane, group):
    return plane ^ (lax.axis_index("blk") // group)


def own_half_kernel(own_ref, out_ref):
    half = out_ref.shape[0]
    own = own_ref[...].T
    for side in range(2):

        @pl.when(lax.rem(lax.axis_index("blk"), 2) == side)
        def _():
            out_ref[...] = own[side * half : (side + 1) * half]


def unit_kernel(own_ref, other_ref, unit_ref):
    half, count = own_ref.shape
    other = other_ref[...].T
    unit_ref[:, :count] = own_ref[...]
    for side in range(2):

        @pl.when(lax.rem(lax.axis_index("blk"), 2) == side)
        def _():
            unit_ref[:, count:] = other[side * half : (side + 1) * half]


def make_unit(own, other, strips):
    count, width = own.shape
    half = width // 2
    if strips == 1:
        kept = call(own_half_kernel, (shape(half, count),), own)[0]
        kept, other = lax.optimization_barrier((kept, other))
        return call(unit_kernel, (shape(half, 2 * count),), kept, other)[0]
    core = lax.rem(lax.axis_index("blk"), 2)
    both = jnp.concatenate([own, other], axis=0).T.reshape(strips, 2, half // strips, 2 * count)
    return lax.dynamic_index_in_dim(both, core, 1, keepdims=False).reshape(half, 2 * count)


def is_inner(z):
    return (z == 1) | (z == 2)


def own_bits():
    core = lax.rem(lax.axis_index("blk"), 2)
    return 1 + core, 2 - core


def late_slot(group):
    return plane_slot(lax.axis_index("shard") ^ 3, group)


def project_part(w_ref, ctx_ref, plane, group):
    return dot(w_ref[plane_slot(plane, group)], ctx_ref[...], NT)


def choose(condition, then, other):
    pl.when(condition)(then)
    pl.when(~condition)(other)


def first_message_kernel(group, own_w, near_w, soon_w, own_ref, other_ref, passing_ref, out_ref):
    count = own_ref.shape[0]
    z, slot, first = lax.axis_index("shard"), late_slot(group), own_bits()[0]

    def share(w_ref):
        for i, ctx_ref in enumerate((own_ref, other_ref)):
            out_ref[:, pl.ds(i * count, count)] = dot(w_ref[...], ctx_ref[...], NT).astype(BF16)

    @pl.when(is_inner(z))
    def _():
        out_ref[...] = passing_ref[...]

    for place, w_ref in (
        (slot == 0, own_w),
        (slot == first, near_w),
        ((slot != 0) & (slot != first), soon_w),
    ):
        pl.when(~is_inner(z) & place)(lambda w_ref=w_ref: share(w_ref))


def all_columns_kernel(group, own_w, near_w, soon_w, last_w, out_ref):
    first, second = own_bits()
    out_ref[0] = own_w[...]
    out_ref[first] = near_w[...]
    far_soon = (late_slot(group) & first) == first
    out_ref[jnp.where(far_soon, 3, second)] = soon_w[...]
    out_ref[jnp.where(far_soon, second, 3)] = last_w[...]


def second_message_kernel(group, w_ref, own_ref, other_ref, passing_ref, out_ref):
    count = own_ref.shape[0]
    z = lax.axis_index("shard")

    @pl.when(is_inner(z))
    def _():
        out_ref[...] = passing_ref[...]

    @pl.when(~is_inner(z))
    def _():
        for i, ctx_ref in enumerate((own_ref, other_ref)):
            part = project_part(w_ref, ctx_ref, z ^ 2, group)
            out_ref[:, pl.ds(i * count, count)] = part.astype(BF16)


def message_kernel(flip, group, w_ref, own_ref, other_ref, past_ref, out_ref):
    count = own_ref.shape[0]
    z = lax.axis_index("shard")
    for i, ctx_ref in enumerate((own_ref, other_ref)):
        at = pl.ds(i * count, count)
        part = project_part(w_ref, ctx_ref, z ^ flip, group)
        past = jnp.where(is_inner(z), past_ref[:, at].astype(F32), 0.0)
        out_ref[:, at] = (part + past).astype(BF16)


def last_project_kernel(group, w_ref, own_ref, other_ref, pair_ref, mid_ref, keep_ref, send_ref):
    count = own_ref.shape[0]
    z = lax.axis_index("shard")
    for i, (ctx_ref, out_ref) in enumerate(((own_ref, keep_ref), (other_ref, send_ref))):
        at = pl.ds(i * count, count)
        part = project_part(w_ref, ctx_ref, z, group) + pair_ref[:, at].astype(F32)
        out_ref[...] = part + jnp.where(is_inner(z), mid_ref[:, at].astype(F32), 0.0)


def layer_out_kernel(residual_ref, keep_ref, other_ref, out_ref):
    half = keep_ref.shape[0]
    core = lax.rem(lax.axis_index("blk"), 2)
    keep, other = keep_ref[...], other_ref[...]
    for side, order in enumerate(((keep, other), (other, keep))):

        @pl.when(core == side)
        def _():
            total = jnp.concatenate(order, axis=0).T
            out_ref[...] = (residual_ref[...].astype(F32) + total).astype(BF16)


def make_layer_out(residual, keep, other, strips):
    count, width = residual.shape
    if strips == 1:
        return call(layer_out_kernel, (shape(count, width),), residual, keep, other)[0]
    core = lax.rem(lax.axis_index("blk"), 2)
    pair = jnp.stack([keep, other]).reshape(2, strips, -1, count)
    pair = jnp.where(core == 0, pair, pair[::-1])
    total = pair.transpose(1, 0, 2, 3).reshape(width, count)
    return (residual.astype(F32) + total.T).astype(BF16)


def late_plane(inner_ref, outer_ref, body):
    z = lax.axis_index("shard")
    pl.when(is_inner(z))(lambda: body(z ^ 3, inner_ref))
    pl.when(~is_inner(z))(lambda: body(z ^ 3, outer_ref))


def d_context_early_kernel(group, unit_ref, near_ref, w_ref, total_ref):
    z = lax.axis_index("shard")
    total_ref[...] = dot(unit_ref[...], w_ref[plane_slot(z, group)], TN)
    total_ref[...] += dot(near_ref[...], w_ref[plane_slot(z ^ 1, group)], TN)


def d_context_late_kernel(group, *refs):
    outer_next, inner_next, inner_far, outer_far, w_ref, total_ref, mine_ref, send_ref = refs
    count = mine_ref.shape[0]
    z = lax.axis_index("shard")

    def finish(next_ref, far_ref):
        part = dot(next_ref[...], w_ref[plane_slot(z ^ 2, group)], TN)
        part = part + dot(far_ref[...], w_ref[plane_slot(z ^ 3, group)], TN)
        mine_ref[...] = total_ref[:count] + part[:count]
        send_ref[...] = (total_ref[count:] + part[count:]).astype(BF16)

    choose(is_inner(z), lambda: finish(inner_next, inner_far), lambda: finish(outer_next, outer_far))


def weight_part(unit_ref, own_ref, other_ref):
    count = own_ref.shape[0]
    part = dot(unit_ref[:, :count], own_ref[...], NN)
    return part + dot(unit_ref[:, count:], other_ref[...], NN)


def first_pair(group):
    core, first = lax.rem(lax.axis_index("blk"), 2), own_bits()[0]
    slot = plane_slot(lax.axis_index("shard"), group)
    return (slot & first) == first, core == 0


def weight_first_kernel(unit_ref, near_ref, own_ref, other_ref, here_ref, near_out):
    here_ref[...] = weight_part(unit_ref, own_ref, other_ref)
    near_out[...] = weight_part(near_ref, own_ref, other_ref)


def weight_early_kernel(group, *refs):
    outer_ref, inner_ref, own_ref, other_ref, here, near, send_a, send_b, beyond = refs
    rows = send_a.shape[0]

    def body(unit_ref):
        beyond[...] = weight_part(unit_ref, own_ref, other_ref)

    def send(block):
        send_a[...] = block[:rows].astype(BF16)
        send_b[...] = block[rows:].astype(BF16)

    choose(is_inner(lax.axis_index("shard")), lambda: body(inner_ref), lambda: body(outer_ref))
    here_goes, with_near = first_pair(group)
    pl.when(here_goes)(lambda: send(here))
    pl.when(~here_goes & with_near)(lambda: send(near))
    pl.when(~here_goes & ~with_near)(lambda: send(beyond))


def weight_late_kernel(group, inner_ref, outer_ref, own_ref, other_ref, near, beyond, send, keep):
    late, first = late_slot(group), own_bits()[0]
    sends = (late & first) == first
    with_near = first_pair(group)[1]

    def send_part(part, rest):
        send[...] = part.astype(BF16)
        keep[...] = rest[...]

    def send_rest(part, rest):
        send[...] = rest[...].astype(BF16)
        keep[...] = part

    def body(plane, unit_ref):
        part = weight_part(unit_ref, own_ref, other_ref)
        for rest, chosen in ((beyond, with_near), (near, ~with_near)):
            pl.when(chosen & sends)(lambda rest=rest: send_part(part, rest))
            pl.when(chosen & ~sends)(lambda rest=rest: send_rest(part, rest))

    late_plane(inner_ref, outer_ref, body)


def half_sum_kernel(group, here, near, beyond, from_a, from_b, late_keep, late_from, send, left):
    rows = from_a.shape[0]
    second = own_bits()[1]
    goes = (late_slot(group) & second) == second
    here_goes, with_near = first_pair(group)

    def add(early_keep):
        for at, early_from in ((pl.ds(0, rows), from_a), (pl.ds(rows, rows), from_b)):
            early_sum = early_keep[at] + early_from[...].astype(F32)
            late_sum = late_keep[at] + late_from[at].astype(F32)
            send[at] = jnp.where(goes, late_sum, early_sum).astype(BF16)
            left[at] = jnp.where(goes, early_sum, late_sum)

    pl.when(~here_goes)(lambda: add(here))
    pl.when(here_goes & with_near)(lambda: add(near))
    pl.when(here_goes & ~with_near)(lambda: add(beyond))


def grad_sum_kernel(scale, left_ref, from_ref, out_ref):
    out_ref[...] = (left_ref[...] + from_ref[...].astype(F32)) * scale


def solution(mesh):
    blk, planes = mesh.shape["blk"], mesh.shape["shard"]
    assert planes == 4
    chips = blk // 2
    strips = chips // planes
    group = 2 * strips

    def swap(value, bit):
        return lax.ppermute(value, "blk", [(i, i ^ bit) for i in range(blk)])

    def core_swap(value, first):
        bits = (1, 2) if first else (2, 1)
        return lax.ppermute(value, "blk", [(i, i ^ (group * bits[i % 2])) for i in range(blk)])

    def pair_swap(value):
        return lax.ppermute(value, "shard", [(0, 1), (1, 0), (2, 3), (3, 2)])

    def mid_swap(value):
        pairs = []
        for b in range(blk):
            pairs += [(b * planes + z, b * planes + (3 - z)) for z in (1, 2)]
            pairs += [(b * planes + z, (b ^ 1) * planes + z) for z in (0, 3)]
        return lax.ppermute(value, ("blk", "shard"), pairs)

    def together(*values):
        return lax.optimization_barrier(values)

    def bound(kernel, *static):
        return lambda *refs: kernel(*static, *refs)

    def per_device(queries, key_rows, values, segment_ids, residual, out_weight, cotangent):
        count, width = queries.shape
        half = width // 2
        position = lax.axis_index("blk") // 2
        unit_flops = 4 * half * count * width
        message = shape(half, 2 * count)

        cot_other = swap(cotangent, 1)

        w_own = out_weight.T
        bit = 1
        while bit < strips:
            there = swap(w_own, 2 * bit)
            upper = (position // bit) % 2
            w_own = jnp.concatenate(
                [jnp.where(upper, there, w_own), jnp.where(upper, w_own, there)], axis=0
            )
            bit *= 2

        w_near = core_swap(w_own, True)
        unit = make_unit(cotangent, cot_other, strips)
        inner_far, near = mid_swap(unit), pair_swap(unit)

        first = own_bits()[0]
        far_soon = (late_slot(group) & first) == first
        w_soon = core_swap(jnp.where(far_soon, w_near, w_own), False)
        w_last = core_swap(jnp.where(far_soon, w_own, w_near), False)
        asked, w_near = together(queries, w_near)
        part = shape(count // 2, width)
        ctx, low, high, probs = call(
            forward_kernel,
            (shape(count, width), part, part, shape(width // HEAD, count, count, dtype=F32)),
            asked,
            key_rows,
            values,
            segment_ids,
            flops=4 * count * count * width,
        )
        near, inner_far, ctx = together(near, inner_far, ctx)
        ctx_other = jnp.concatenate([swap(low, 1), swap(high, 1)], axis=0)

        inner_next = mid_swap(near)
        out = call(
            bound(first_message_kernel, group),
            (message,),
            w_own,
            w_near,
            w_soon,
            ctx,
            ctx_other,
            inner_far,
            flops=unit_flops,
        )[0]
        pair_two = pair_swap(out)
        w_all = call(
            bound(all_columns_kernel, group),
            (shape(planes, half, width),),
            w_own,
            w_near,
            w_soon,
            w_last,
        )[0]
        sources = (w_all, ctx, ctx_other)
        d_ctx_early = call(
            bound(d_context_early_kernel, group),
            (shape(2 * count, width, dtype=F32),),
            unit,
            near,
            w_all,
            flops=2 * unit_flops,
        )[0]
        block, rest = shape(half, width), shape(half, width, dtype=F32)
        here_part, near_part = call(
            weight_first_kernel, (rest, rest), unit, near, ctx, ctx_other, flops=2 * unit_flops
        )
        inner_next, d_ctx_early, here_part = together(inner_next, d_ctx_early, here_part)

        out = call(
            bound(second_message_kernel, group), (message,), *sources, inner_next, flops=unit_flops
        )[0]
        pair_three = pair_swap(out)
        out, pair_two = together(out, pair_two)
        out = call(
            bound(message_kernel, 2, group), (message,), *sources, pair_two, flops=unit_flops
        )[0]
        mid_three = mid_swap(out)
        piece = shape(half // 2, width)
        early_send_a, early_send_b, beyond_part = call(
            bound(weight_early_kernel, group),
            (piece, piece, rest),
            pair_two,
            inner_next,
            ctx,
            ctx_other,
            here_part,
            near_part,
            flops=unit_flops,
        )
        early_from_a, early_from_b = core_swap(early_send_a, True), core_swap(early_send_b, True)
        pair_three, beyond_part = together(pair_three, beyond_part)

        late_send, late_keep = call(
            bound(weight_late_kernel, group),
            (block, rest),
            inner_far,
            pair_three,
            ctx,
            ctx_other,
            near_part,
            beyond_part,
            flops=unit_flops,
        )
        late_from = core_swap(late_send, True)
        mid_three, late_send = together(mid_three, late_send)
        out = call(
            bound(message_kernel, 1, group), (message,), *sources, mid_three, flops=unit_flops
        )[0]
        pair_four = pair_swap(out)
        pair_three, early_from_a, early_from_b, out = together(pair_three, early_from_a, early_from_b, out)
        out = call(
            bound(message_kernel, 3, group), (message,), *sources, pair_three, flops=unit_flops
        )[0]
        mid_four = mid_swap(out)
        d_ctx_early, out = together(d_ctx_early, out)
        mine, send = call(
            bound(d_context_late_kernel, group),
            (shape(count, width, dtype=F32), shape(count, width)),
            pair_two,
            inner_next,
            inner_far,
            pair_three,
            w_all,
            d_ctx_early,
            flops=2 * unit_flops,
        )
        d_ctx_other = swap(send, 1)
        late_from, out = together(late_from, out)
        send, left = call(
            bound(half_sum_kernel, group),
            (block, rest),
            here_part,
            near_part,
            beyond_part,
            early_from_a,
            early_from_b,
            late_keep,
            late_from,
        )
        second_from = core_swap(send, False)

        pair_four, mid_four = together(pair_four, mid_four)
        keep, send = call(
            bound(last_project_kernel, group),
            (shape(half, count, dtype=F32),) * 2,
            *sources,
            pair_four,
            mid_four,
            flops=unit_flops,
        )
        last_other = swap(send, 1)
        mine, keep = together(mine, keep)
        d_queries, d_keys, d_values = call(
            backward_kernel,
            (shape(count, width),) * 3,
            queries,
            key_rows,
            values,
            probs,
            mine,
            d_ctx_other,
            flops=10 * count * count * width,
        )
        layer_out = make_layer_out(residual, keep, last_other, strips)
        left, layer_out = together(left, layer_out)
        total = call(
            bound(grad_sum_kernel, 1.0 / math.sqrt(count * blk)),
            (shape(half, width, dtype=F32),),
            left,
            second_from,
        )[0]
        bit = strips // 2
        while bit >= 1:
            lower, upper = jnp.split(total, 2, axis=0)
            right = (position // bit) % 2
            sent = jnp.where(right, lower, upper)
            total = jnp.where(right, upper, lower) + swap(sent, 2 * bit)
            bit //= 2

        return layer_out, total, d_queries, d_keys, d_values

    spread = P("blk", "shard")
    return jax.shard_map(
        per_device,
        mesh=mesh,
        in_specs=(spread, spread, spread, P("blk", None), spread, P("shard", "blk"), spread),
        out_specs=(spread,) * 5,
        check_vma=False,
    )
```
